32 devices in a mesh: elem: 8 (over z, y), grp: 4 (over x, core).
Axes of the slice: x: 2, y: 2, z: 4, core: 2. Of those that a mesh axis runs over, the one named last changes fastest.
Arguments:
- basis_values: bfloat16 [8, 1024, 8192], P('elem', 'grp'), may hold values from -0.0625 to 0.0625
- basis_derivs: bfloat16 [8, 1024, 8192], P('elem', 'grp'), may hold values from -0.0625 to 0.0625
- potential: float32 [8, 8192], P('elem', 'grp'), may hold values from 0.5 to 2
- hop_blocks: bfloat16 [8, 4, 1024, 1024], P('elem', None, 'grp'), may hold values from -0.1875 to 0.1875
- coeffs: bfloat16 [8, 1024, 4096], P('elem', None, 'grp'), may hold values from -6 to 6
- counts: int32 [8], replicated, may hold values from 256 to 1024, as said below
- neighbours: int32 [8, 4], replicated, may hold values from 0 to 7, as said below
Outputs:
- applied_bands: float32 [8, 1024, 4096], P('elem', None, 'grp')
The draws below stay inside these ranges and needn't reach their ends.
Inputs may be any that keep to these rules, and one draw needn't show every extreme that they name: `counts`: count of live basis functions of each element; some element has exactly 1024 and some exactly 256. `neighbours`: four distinct elements, none the element itself.
All inputs are finite; a program needn't handle non-finite values.
Results may differ from the reference program's by a relative error of at most 0.0022.
Values may be sent and summed in bfloat16 or wider, within the bound.
A program may use at most 192 MiB of HBM per device.

```python
import jax
import jax.numpy as jnp
from jax import lax

MAXB = 1024
BANDS = 4096
NEIGH = 4
P_SIZE = 8192
NELEM = 8


def draw_counts(key, part):
    first_key, second_key = jax.random.split(key)
    raw_counts = jax.random.randint(first_key, (NELEM,), MAXB // 4, MAXB + 1)
    spots = jax.random.permutation(second_key, NELEM)
    raw_counts = raw_counts.at[spots[0]].set(MAXB).at[spots[1]].set(MAXB // 4)
    return raw_counts.astype(jnp.int32)


def draw_neighbours(key, part):
    chain_order = jax.random.permutation(key, NELEM).astype(jnp.int32)
    places = jnp.argsort(chain_order, stable=True).astype(jnp.int32)
    offsets = jnp.array([-2, -1, 1, 2], dtype=jnp.int32)
    return chain_order[(places[:, None] + offsets[None, :]) % NELEM].astype(jnp.int32)


def block_scale(rng, dims, pieces, least, top_value):
    def one(position, blocks):
        draws = jax.random.uniform(jax.random.fold_in(jax.random.fold_in(rng, 6), position), (blocks,), jnp.float32, least / len(pieces), top_value / len(pieces))
        return jnp.repeat(jnp.exp(draws), dims[position] // blocks).reshape((-1,) + (1,) * (len(dims) - position - 1))

    gain = one(*pieces[0])
    for cut in pieces[1:]:
        gain = gain * one(*cut)
    return gain


def scatter_about(rng, dims, spread, reach, pieces=(), kind=jnp.bfloat16):
    drawn = spread * jax.random.normal(rng, dims, jnp.float32)
    if pieces:
        drawn = drawn * block_scale(rng, dims, pieces, -0.22, 0.18)
    return jnp.clip(drawn, -reach, reach).astype(kind)


def setup_inputs(seed: int = 0) -> dict:
    streams_of = jax.random.split(jax.random.key(seed), 8)
    return {
        "basis_values": scatter_about(streams_of[0], (NELEM, MAXB, P_SIZE), P_SIZE ** -0.5, 0.0625, ((0, 8), (1, 4))),
        "basis_derivs": scatter_about(streams_of[1], (NELEM, MAXB, P_SIZE), P_SIZE ** -0.5, 0.0625, ((0, 8), (1, 4))),
        "potential": jnp.clip(0.5 + 1.5 * jax.random.uniform(streams_of[2], (NELEM, P_SIZE), jnp.float32) ** block_scale(streams_of[2], (NELEM, P_SIZE), ((0, 8), (1, 4)), -0.2, 0.2), 0.5, 2.0),
        "hop_blocks": scatter_about(streams_of[3], (NELEM, NEIGH, MAXB, MAXB), MAXB ** -0.5, 0.1875, ((0, 8), (2, 4))),
        "coeffs": scatter_about(streams_of[4], (NELEM, MAXB, BANDS), 1.0, 6.0, ((0, 8), (2, 4))),
        "counts": draw_counts(jax.random.fold_in(streams_of[7], 71), 0),
        "neighbours": draw_neighbours(jax.random.fold_in(streams_of[7], 71), 0),
    }


def reference(basis_values, basis_derivs, potential, hop_blocks, coeffs, counts, neighbours):
    row_ids = jnp.arange(MAXB, dtype=jnp.int32)
    live_rows = row_ids[None, :] < counts[:, None]
    masked = jnp.where(live_rows[:, :, None], coeffs, jnp.zeros_like(coeffs))

    def element_term(element):
        values_here = basis_values[element]
        derivs_here = basis_derivs[element]
        weighted = (potential[element][None, :] * values_here.astype(jnp.float32)).astype(jnp.bfloat16)
        assembled = 0.5 * jnp.dot(derivs_here, derivs_here.T, preferred_element_type=jnp.float32)
        assembled = assembled + jnp.dot(values_here, weighted.T, preferred_element_type=jnp.float32)
        assembled_low = assembled.astype(jnp.bfloat16)
        applied = jnp.dot(assembled_low, masked[element], preferred_element_type=jnp.float32)
        for which in range(NEIGH):
            applied = applied + jnp.dot(hop_blocks[element, which], masked[neighbours[element, which]], preferred_element_type=jnp.float32)
        return jnp.where(live_rows[element][:, None], applied, jnp.zeros_like(applied))

    return lax.map(element_term, jnp.arange(NELEM, dtype=jnp.int32))
```

```python
import functools

import jax
import jax.numpy as jnp
from jax import lax
from jax.experimental import pallas as pl
from jax.experimental.pallas import tpu as pltpu
from jax.sharding import PartitionSpec as P


def local(basis_values, basis_derivs, potential, hop_blocks, coeffs, counts, neighbours):
    values_slab, derivs_slab = (
        lax.all_to_all(basis_values, "grp", split_axis=2, concat_axis=1, tiled=True),
        lax.all_to_all(basis_derivs, "grp", split_axis=2, concat_axis=1, tiled=True),
    )
    values_slab = values_slab[0]
    derivs_slab = derivs_slab[0]
    weighted = (potential[0][None, :] * values_slab.astype(jnp.float32)).astype(jnp.bfloat16)
    partial_value = 0.5 * jnp.einsum(
        "ip,jp->ij", derivs_slab, derivs_slab, preferred_element_type=jnp.float32
    )
    partial_value = partial_value + jnp.einsum(
        "ip,jp->ij", values_slab, weighted, preferred_element_type=jnp.float32
    )
    element = lax.axis_index("elem")
    width = coeffs.shape[1]
    row_ids = jnp.arange(width, dtype=jnp.int32)
    live_rows = row_ids < counts[element]
    own_coeffs = jnp.where(live_rows[:, None], coeffs[0], jnp.zeros_like(coeffs[0]))
    near_ids = neighbours[element]
    initial = jnp.zeros((near_ids.shape[0], width, coeffs.shape[2]), jnp.bfloat16)
    pieces = lax.all_gather(own_coeffs[None], "elem", axis=0, tiled=True)
    inside = (near_ids >= 0) & (near_ids < pieces.shape[0])
    clipped = jnp.clip(near_ids, 0, pieces.shape[0] - 1)
    picked = jnp.take(pieces, clipped, axis=0)
    near_coeffs = jnp.where(inside[:, None, None], picked, initial)
    assembled_low = lax.psum(partial_value, "grp").astype(jnp.bfloat16)
    applied = jnp.dot(assembled_low, own_coeffs, preferred_element_type=jnp.float32)
    applied = applied + jnp.einsum(
        "krm,kmb->rb",
        lax.all_gather(hop_blocks, "grp", axis=2, tiled=True)[0],
        near_coeffs,
        preferred_element_type=jnp.float32,
    )
    result = jnp.where(live_rows[:, None], applied, jnp.zeros_like(applied))
    return result[None]


NT = (((1,), (1,)), ((), ()))
PIECES = 4
CHUNKS = 6


def exchange_kernel(
    values, derivs, pot, hop, coeffs,
    near, hop_all, diag, off,
    vbuf, dbuf, vbuf2, dbuf2, potbuf, acc_d, acc_o, got_d, got_o, got_x, sum_o, low_d, low_o,
    load_sem, pair_send, pair_recv, slab_send, slab_recv, pot_sem, red_send, red_recv,
    diag_send, diag_recv, off_send, off_recv, hop_send, hop_recv,
    right_send, left_send, y_send, near_recv,
):
    e = lax.axis_index("elem")
    g = lax.axis_index("grp")
    z, y = e // 2, e % 2
    x, c = g // 2, g % 2
    partner = {"grp": 2 * x + 1 - c}
    across = {"grp": 2 * (1 - x) + c}
    beyond = {"grp": 2 * (1 - x) + 1 - c}
    y_dev = {"elem": 2 * z + 1 - y}
    right = {"elem": e + 2}
    left = {"elem": e - 2}
    depth = 4
    rows, width = coeffs.shape
    part = rows * 9 // 64 // 16 * 16
    n_rows, slab = vbuf.shape[1], vbuf.shape[2]
    piece = slab // PIECES
    other_slab = 2 * (1 - x) + c

    def remote(src, dst, ss, rs, dev):
        return pltpu.make_async_remote_copy(
            src_ref=src, dst_ref=dst, send_sem=ss, recv_sem=rs,
            device_id=dev, device_id_type=pl.DeviceIdType.MESH,
        )

    barrier = pltpu.get_barrier_semaphore()
    for dev in (partner, across, beyond, y_dev):
        pl.semaphore_signal(barrier, inc=1, device_id=dev, device_id_type=pl.DeviceIdType.MESH)

    @pl.when(z < depth - 1)
    def _():
        pl.semaphore_signal(barrier, inc=1, device_id=right, device_id_type=pl.DeviceIdType.MESH)

    @pl.when(z > 0)
    def _():
        pl.semaphore_signal(barrier, inc=1, device_id=left, device_id_type=pl.DeviceIdType.MESH)

    pl.semaphore_wait(barrier, 4 + (z + depth - 2) // (depth - 1) + (2 * depth - 3 - z) // (depth - 1))

    def points(which, start, size):
        return pl.ds(pl.multiple_of(which * slab + start, 128), size)

    def slab_copy(core, arr, k, mine):
        src = (values, derivs)[arr].at[:, points(2 * (1 - x) + core, k * piece, piece)]
        row = g if mine else 2 * (1 - x) + core
        dst = (vbuf, dbuf)[arr].at[row, :, pl.ds(k * piece, piece)]
        return remote(
            src, dst, slab_send.at[core, arr, k],
            slab_recv.at[c if mine else core, arr, k], {"grp": 2 * (1 - x) + core},
        )

    def pair_copy(which, arr, mine):
        ref = (values, derivs)[arr]
        their = 1 - c if mine else c
        src = ref.at[:, points(2 * x + their if which == 0 else 2 * (1 - x) + their, 0, slab)]
        if which == 0:
            dst = (vbuf, dbuf)[arr].at[g if mine else 2 * x + 1 - c]
        else:
            dst = (vbuf2, dbuf2)[arr].at[c if mine else 1 - c]
        return remote(src, dst, pair_send.at[which, arr], pair_recv.at[which, arr], partner)

    def pot_copy():
        return remote(pot, potbuf.at[1], pot_sem.at[0], pot_sem.at[1], across)

    pot_copy().start()
    for k in range(PIECES):
        for arr in range(2):
            for core in range(2):
                slab_copy(core, arr, k, True).start()

    def rows_of(k):
        if k < CHUNKS:
            return pl.ds(k * part, part)
        return pl.ds(CHUNKS * part, rows - CHUNKS * part)

    def near_copy(sems, src_e, k, dev, own=False):
        src = coeffs.at[rows_of(k)] if own else near.at[src_e, rows_of(k)]
        return remote(src, near.at[src_e, rows_of(k)], sems.at[src_e, k], near_recv.at[src_e, k], dev)

    def to_right(src_e, k, act, own=False):
        @pl.when(z < depth - 1)
        def _():
            act(near_copy(right_send, src_e, k, right, own))

    def to_left(src_e, k, act, own=False):
        @pl.when(z > 0)
        def _():
            act(near_copy(left_send, src_e, k, left, own))

    def start(copy):
        copy.start()

    def wait_send(copy):
        copy.wait_send()

    near_copy(y_send, e, CHUNKS, y_dev, True).start()
    for k in range(CHUNKS + 1):
        to_right(e, k, start, True)
        to_left(e, k, start, True)
        if k < CHUNKS:
            near_copy(y_send, e, k, y_dev, True).start()

    loads = []

    def load(src, dst):
        copy = pltpu.make_async_copy(src, dst, load_sem.at[len(loads)])
        copy.start()
        loads.append(copy)

    for arr in range(2):
        for which in range(2):
            pair_copy(which, arr, True).start()
    for arr in range(2):
        ref = (values, derivs)[arr]
        load(ref.at[:, points(g, 0, slab)], (vbuf, dbuf)[arr].at[g])
        load(ref.at[:, points(other_slab, 0, slab)], (vbuf2, dbuf2)[arr].at[c])
    load(pot, potbuf.at[0])
    load(coeffs, near.at[e])
    load(hop, hop_all.at[:, g])
    n_hop = hop.shape[0]

    def hop_pair(mine):
        return remote(
            hop, hop_all.at[:, g if mine else 2 * x + 1 - c], hop_send.at[0], hop_recv.at[0], partner
        )

    def hop_across(k, mine):
        return remote(
            hop.at[k], hop_all.at[k, g if mine else 2 * (1 - x) + c],
            hop_send.at[1 + k], hop_recv.at[1 + k], across,
        )

    def hop_relay(k, mine):
        row = 2 * (1 - x) + (c if mine else 1 - c)
        ref = hop_all.at[k, row]
        return remote(ref, ref, hop_send.at[1 + n_hop + k], hop_recv.at[1 + n_hop + k], partner)

    hop_pair(True).start()

    def product(v_low, d_low, v_high, d_high, weight):
        weighted = (weight * v_high.astype(jnp.float32)).astype(jnp.bfloat16)
        out = 0.5 * lax.dot_general(d_low, d_high, NT, preferred_element_type=jnp.float32)
        return out + lax.dot_general(v_low, weighted, NT, preferred_element_type=jnp.float32)

    half = 2 * n_rows

    def two(ref, first, cols):
        return ref[pl.ds(first, 2), :, cols].reshape(half, piece)

    def diag_product():
        for copy in loads[:5]:
            copy.wait()
        for arr in range(2):
            for which in range(2):
                pair_copy(which, arr, False).wait_recv()
        pot_copy().wait_recv()
        acc_d[...] = jnp.zeros_like(acc_d)

        @pl.loop(0, PIECES)
        def _(k):
            cols = pl.ds(pl.multiple_of(k * piece, 128), piece)
            for vb, db, first, which in ((vbuf, dbuf, 2 * x, 0), (vbuf2, dbuf2, 0, 1)):
                v = two(vb, first, cols)
                d = two(db, first, cols)
                acc_d[...] += product(v, d, v, d, potbuf[which, 0:1, cols]).reshape(acc_d.shape)

        remote(acc_d.at[1 - c], got_d, red_send.at[0], red_recv.at[0], partner).start()

    def diag_finish():
        remote(acc_d.at[1 - c], got_d, red_send.at[0], red_recv.at[0], partner).wait_recv()
        low_d[...] = (acc_d[c] + got_d[...]).astype(jnp.bfloat16)
        load(low_d, diag.at[g])
        remote(low_d, diag.at[g], diag_send.at[0], diag_recv.at[0], partner).start()
        remote(low_d, diag.at[g], diag_send.at[1], diag_recv.at[1], across).start()

    def diag_relay(mine):
        ref = diag.at[2 * (1 - x) + (c if mine else 1 - c)]
        return remote(ref, ref, diag_send.at[2], diag_recv.at[2], partner)

    def diag_forward():
        remote(low_d, diag.at[2 * (1 - x) + c], diag_send.at[1], diag_recv.at[1], across).wait_recv()
        diag_relay(True).start()

    def off_piece(k):
        for arr in range(2):
            for core in range(2):
                slab_copy(core, arr, k, False).wait_recv()
        cols = pl.ds(k * piece, piece)
        term = product(
            two(vbuf, 0, cols), two(dbuf, 0, cols), two(vbuf, 2, cols), two(dbuf, 2, cols),
            potbuf[0, 0:1, cols],
        ).reshape(acc_o.shape)
        if k == 0:
            acc_o[...] = term
        else:
            acc_o[...] += term
        if k == PIECES - 2:
            hop_across(0, True).start()
            hop_across(1, True).start()
        if k == PIECES - 1:
            remote(acc_o.at[1 - c], got_o, red_send.at[1], red_recv.at[1], partner).start()

    def off_sum():
        remote(acc_o.at[1 - c], got_o, red_send.at[1], red_recv.at[1], partner).wait_recv()
        sum_o[...] = acc_o[c] + got_o[...]
        remote(sum_o, got_x, red_send.at[2], red_recv.at[2], across).start()
        hop_across(2, True).start()
        hop_across(3, True).start()

    def off_finish():
        remote(sum_o, got_x, red_send.at[2], red_recv.at[2], across).wait_recv()
        low_o[...] = (sum_o[...] + got_x[...]).astype(jnp.bfloat16)
        load(low_o, off.at[c])
        remote(low_o, off.at[c], off_send, off_recv, partner).start()

    def hop_forward(k):
        hop_across(k, False).wait_recv()
        hop_relay(k, True).start()

    plan = {
        (1, 0): [diag_product],
        (1, 1): [diag_finish],
        (1, 2): [functools.partial(off_piece, 0)],
        (1, 5): [functools.partial(off_piece, 1)],
        (2, 0): [diag_forward],
        (2, 2): [functools.partial(off_piece, 2)],
        (2, 5): [functools.partial(off_piece, 3)],
        (3, 0): [off_sum],
        (3, 2): [functools.partial(hop_forward, 0), off_finish],
        (3, 3): [functools.partial(hop_forward, 1)],
    }

    nbr = 2 * z + 1 - y
    near_copy(y_send, nbr, CHUNKS, y_dev).wait_recv()
    to_right(nbr, CHUNKS, start)
    to_left(nbr, CHUNKS, start)

    for d in range(1, depth):
        for k in range(CHUNKS):
            @pl.when(z >= d)
            def _():
                near_copy(right_send, e - 2 * d, k, right).wait_recv()
                to_right(e - 2 * d, k, start)
                near_copy(y_send, e - 2 * d, k, y_dev).start()

            @pl.when(z + d < depth)
            def _():
                near_copy(left_send, e + 2 * d, k, left).wait_recv()
                to_left(e + 2 * d, k, start)
                near_copy(y_send, e + 2 * d, k, y_dev).start()

            for step in plan.get((d, k), ()):
                step()
        for base in (e, nbr):
            @pl.when(z >= d)
            def _():
                near_copy(right_send, base - 2 * d, CHUNKS, right).wait_recv()
                to_right(base - 2 * d, CHUNKS, start)

            @pl.when(z + d < depth)
            def _():
                near_copy(left_send, base + 2 * d, CHUNKS, left).wait_recv()
                to_left(base + 2 * d, CHUNKS, start)

    hop_forward(2)
    hop_forward(3)

    hop_pair(False).wait_recv()
    for k in range(n_hop):
        hop_relay(k, False).wait_recv()
    remote(low_d, diag.at[2 * x + 1 - c], diag_send.at[0], diag_recv.at[0], partner).wait_recv()
    diag_relay(False).wait_recv()
    remote(low_o, off.at[1 - c], off_send, off_recv, partner).wait_recv()

    @pl.loop(0, depth)
    def _(zz):
        for k in range(CHUNKS):
            near_copy(y_send, 2 * zz + 1 - y, k, y_dev).wait_recv()

    for copy in loads[5:]:
        copy.wait()
    pot_copy().wait_send()
    for arr in range(2):
        for which in range(2):
            pair_copy(which, arr, True).wait_send()
        for core in range(2):
            for k in range(PIECES):
                slab_copy(core, arr, k, True).wait_send()
    hop_pair(True).wait_send()
    for k in range(n_hop):
        hop_across(k, True).wait_send()
        hop_relay(k, True).wait_send()
    remote(acc_d.at[1 - c], got_d, red_send.at[0], red_recv.at[0], partner).wait_send()
    remote(acc_o.at[1 - c], got_o, red_send.at[1], red_recv.at[1], partner).wait_send()
    remote(sum_o, got_x, red_send.at[2], red_recv.at[2], across).wait_send()
    remote(low_d, diag.at[g], diag_send.at[0], diag_recv.at[0], partner).wait_send()
    remote(low_d, diag.at[g], diag_send.at[1], diag_recv.at[1], across).wait_send()
    diag_relay(True).wait_send()
    remote(low_o, off.at[c], off_send, off_recv, partner).wait_send()
    near_copy(y_send, e, CHUNKS, y_dev).wait_send()

    @pl.loop(0, depth)
    def _(zz):
        src = 2 * zz + y
        for k in range(CHUNKS):
            near_copy(y_send, src, k, y_dev).wait_send()

        @pl.when(zz <= z)
        def _():
            for k in range(CHUNKS + 1):
                to_right(src, k, wait_send)
            to_right(2 * zz + 1 - y, CHUNKS, wait_send)

        @pl.when(zz >= z)
        def _():
            for k in range(CHUNKS + 1):
                to_left(src, k, wait_send)
            to_left(2 * zz + 1 - y, CHUNKS, wait_send)


def apply_kernel(ids, live, blocks_a, blocks_h, near, out):
    step = pl.program_id(0)
    rows = lax.broadcasted_iota(jnp.int32, near.shape, 0)
    picked = jnp.where(rows < live[step], near[...], jnp.zeros_like(near))

    @pl.when(step == 0)
    def _():
        out[...] = jnp.dot(blocks_a[...], picked, preferred_element_type=jnp.float32)

    @pl.when(step > 0)
    def _():
        out[...] += jnp.dot(blocks_h[...], picked, preferred_element_type=jnp.float32)

    @pl.when(step == pl.num_programs(0) - 1)
    def _():
        ids_out = lax.broadcasted_iota(jnp.int32, out.shape, 0)
        out[...] = jnp.where(ids_out < live[0], out[...], 0.0)


def local_kernels(basis_values, basis_derivs, potential, hop_blocks, coeffs, counts, neighbours):
    n_elem = counts.shape[0]
    width, bands = coeffs.shape[1:]
    n_rows, n_points = basis_values.shape[1:]
    slab = potential.shape[1]
    n_hop = hop_blocks.shape[1]
    n_grp = width // n_rows
    half = 2 * n_rows
    bf16, f32 = jnp.bfloat16, jnp.float32
    anywhere = pl.BlockSpec(memory_space=pl.ANY)
    dma = pltpu.SemaphoreType.DMA
    vmem = pltpu.VMEM
    flops = 2 * half * half * 3 * 2 * slab
    near, hop_all, diag, off = pl.pallas_call(
        exchange_kernel,
        out_shape=(
            jax.ShapeDtypeStruct((n_elem, width, bands), bf16),
            jax.ShapeDtypeStruct((n_hop, n_grp, n_rows, width), bf16),
            jax.ShapeDtypeStruct((n_grp, n_rows, half), bf16),
            jax.ShapeDtypeStruct((2, n_rows, half), bf16),
        ),
        in_specs=[anywhere] * 5,
        out_specs=(anywhere,) * 4,
        scratch_shapes=[
            vmem((n_grp, n_rows, slab), bf16), vmem((n_grp, n_rows, slab), bf16),
            vmem((2, n_rows, slab), bf16), vmem((2, n_rows, slab), bf16),
            vmem((2, 8, slab), f32),
            vmem((2, n_rows, half), f32), vmem((2, n_rows, half), f32),
            vmem((n_rows, half), f32), vmem((n_rows, half), f32),
            vmem((n_rows, half), f32), vmem((n_rows, half), f32),
            vmem((n_rows, half), bf16), vmem((n_rows, half), bf16),
            dma((9,)), dma((2, 2)), dma((2, 2)), dma((2, 2, PIECES)), dma((2, 2, PIECES)), dma((2,)),
            dma((3,)), dma((3,)), dma((3,)), dma((3,)), dma, dma,
            dma((1 + 2 * n_hop,)), dma((1 + 2 * n_hop,)),
            dma((n_elem, CHUNKS + 1)), dma((n_elem, CHUNKS + 1)),
            dma((n_elem, CHUNKS + 1)), dma((n_elem, CHUNKS + 1)),
        ],
        compiler_params=pltpu.CompilerParams(
            collective_id=0, has_side_effects=True, vmem_limit_bytes=50 * 2 ** 20
        ),
        cost_estimate=pl.CostEstimate(flops=flops, bytes_accessed=2 ** 26, transcendentals=0),
        name="exchange",
    )(
        basis_values[0], basis_derivs[0], jnp.broadcast_to(potential, (8, slab)),
        hop_blocks[0], coeffs[0],
    )
    off = off.reshape(half, half)
    diag = diag.reshape(2, half, half)
    assembled = jnp.concatenate(
        [jnp.concatenate([diag[0], off], 1), jnp.concatenate([off.T, diag[1]], 1)], 0
    )
    element = lax.axis_index("elem")
    ids = jnp.concatenate([element[None].astype(jnp.int32), neighbours[element]])
    live = counts[ids]
    out = pl.pallas_call(
        apply_kernel,
        out_shape=jax.ShapeDtypeStruct((width, bands), f32),
        grid_spec=pltpu.PrefetchScalarGridSpec(
            num_scalar_prefetch=2,
            grid=(1 + n_hop,),
            in_specs=[
                pl.BlockSpec((width, width), lambda s, ids, live: (0, 0)),
                pl.BlockSpec((None, width, width), lambda s, ids, live: (jnp.maximum(s - 1, 0), 0, 0)),
                pl.BlockSpec((None, width, bands), lambda s, ids, live: (ids[s], 0, 0)),
            ],
            out_specs=pl.BlockSpec((width, bands), lambda s, ids, live: (0, 0)),
        ),
        compiler_params=pltpu.CompilerParams(vmem_limit_bytes=50 * 2 ** 20),
        cost_estimate=pl.CostEstimate(
            flops=2 * (1 + n_hop) * width * width * bands, bytes_accessed=2 ** 25, transcendentals=0
        ),
        name="apply",
    )(ids, live, assembled, hop_all.reshape(n_hop, width, width), near)
    return out[None]


def solution(mesh):
    placed = (
        P("elem", "grp", None),
        P("elem", "grp", None),
        P("elem", "grp"),
        P("elem", None, "grp", None),
        P("elem", None, "grp"),
        P(),
        P(),
    )
    fits = mesh.shape["elem"] == 8 and mesh.shape["grp"] == 4
    return jax.shard_map(
        local_kernels if fits else local,
        mesh=mesh, in_specs=placed, out_specs=P("elem", None, "grp"), check_vma=False,
    )
```

```python
import functools

import jax
import jax.numpy as jnp
from jax import lax
from jax.experimental import pallas as pl
from jax.experimental.pallas import tpu as pltpu
from jax.sharding import PartitionSpec as P


def local(basis_values, basis_derivs, potential, hop_blocks, coeffs, counts, neighbours):
    values_slab, derivs_slab = (
        lax.all_to_all(basis_values, "grp", split_axis=2, concat_axis=1, tiled=True),
        lax.all_to_all(basis_derivs, "grp", split_axis=2, concat_axis=1, tiled=True),
    )
    values_slab = values_slab[0]
    derivs_slab = derivs_slab[0]
    weighted = (potential[0][None, :] * values_slab.astype(jnp.float32)).astype(jnp.bfloat16)
    partial_value = 0.5 * jnp.einsum(
        "ip,jp->ij", derivs_slab, derivs_slab, preferred_element_type=jnp.float32
    )
    partial_value = partial_value + jnp.einsum(
        "ip,jp->ij", values_slab, weighted, preferred_element_type=jnp.float32
    )
    element = lax.axis_index("elem")
    width = coeffs.shape[1]
    row_ids = jnp.arange(width, dtype=jnp.int32)
    live_rows = row_ids < counts[element]
    own_coeffs = jnp.where(live_rows[:, None], coeffs[0], jnp.zeros_like(coeffs[0]))
    near_ids = neighbours[element]
    initial = jnp.zeros((near_ids.shape[0], width, coeffs.shape[2]), jnp.bfloat16)
    pieces = lax.all_gather(own_coeffs[None], "elem", axis=0, tiled=True)
    inside = (near_ids >= 0) & (near_ids < pieces.shape[0])
    clipped = jnp.clip(near_ids, 0, pieces.shape[0] - 1)
    picked = jnp.take(pieces, clipped, axis=0)
    near_coeffs = jnp.where(inside[:, None, None], picked, initial)
    assembled_low = lax.psum(partial_value, "grp").astype(jnp.bfloat16)
    applied = jnp.dot(assembled_low, own_coeffs, preferred_element_type=jnp.float32)
    applied = applied + jnp.einsum(
        "krm,kmb->rb",
        lax.all_gather(hop_blocks, "grp", axis=2, tiled=True)[0],
        near_coeffs,
        preferred_element_type=jnp.float32,
    )
    result = jnp.where(live_rows[:, None], applied, jnp.zeros_like(applied))
    return result[None]


NT = (((1,), (1,)), ((), ()))
PIECES = 4
CHUNKS = 6


def hamiltonian_kernel(
    values, derivs, pot, hop, coeffs, counts, neighbours, out,
    near, hop_all, amat, acc,
    vbuf, dbuf, vbuf2, dbuf2, potbuf, acc_d, acc_o, got_d, got_o, sum_o, low_o, got_x,
    load_sem, pair_send, pair_recv, slab_send, slab_recv, pot_sem, red_send, red_recv,
    diag_send, diag_recv, off_send, off_recv, hop_send, hop_recv,
    right_send, left_send, y_send, near_recv, out_sem,
):
    e = lax.axis_index("elem")
    g = lax.axis_index("grp")
    z, y = e // 2, e % 2
    x, c = g // 2, g % 2
    partner = {"grp": 2 * x + 1 - c}
    across = {"grp": 2 * (1 - x) + c}
    beyond = {"grp": 2 * (1 - x) + 1 - c}
    y_dev = {"elem": 2 * z + 1 - y}
    right = {"elem": e + 2}
    left = {"elem": e - 2}
    depth = 4
    rows, width = coeffs.shape
    part = rows * 9 // 64 // 16 * 16
    n_rows, slab = vbuf.shape[1], vbuf.shape[2]
    piece = slab // PIECES
    other_slab = 2 * (1 - x) + c

    def remote(src, dst, ss, rs, dev):
        return pltpu.make_async_remote_copy(
            src_ref=src, dst_ref=dst, send_sem=ss, recv_sem=rs,
            device_id=dev, device_id_type=pl.DeviceIdType.MESH,
        )

    barrier = pltpu.get_barrier_semaphore()
    for dev in (partner, across, beyond, y_dev):
        pl.semaphore_signal(barrier, inc=1, device_id=dev, device_id_type=pl.DeviceIdType.MESH)

    @pl.when(z < depth - 1)
    def _():
        pl.semaphore_signal(barrier, inc=1, device_id=right, device_id_type=pl.DeviceIdType.MESH)

    @pl.when(z > 0)
    def _():
        pl.semaphore_signal(barrier, inc=1, device_id=left, device_id_type=pl.DeviceIdType.MESH)

    pl.semaphore_wait(barrier, 4 + (z + depth - 2) // (depth - 1) + (2 * depth - 3 - z) // (depth - 1))

    def points(which, start, size):
        return pl.ds(pl.multiple_of(which * slab + start, 128), size)

    def slab_copy(core, arr, k, mine):
        src = (values, derivs)[arr].at[:, points(2 * (1 - x) + core, k * piece, piece)]
        row = g if mine else 2 * (1 - x) + core
        dst = (vbuf, dbuf)[arr].at[row, :, pl.ds(k * piece, piece)]
        return remote(
            src, dst, slab_send.at[core, arr, k],
            slab_recv.at[c if mine else core, arr, k], {"grp": 2 * (1 - x) + core},
        )

    def pair_copy(which, arr, mine):
        ref = (values, derivs)[arr]
        their = 1 - c if mine else c
        src = ref.at[:, points(2 * x + their if which == 0 else 2 * (1 - x) + their, 0, slab)]
        if which == 0:
            dst = (vbuf, dbuf)[arr].at[g if mine else 2 * x + 1 - c]
        else:
            dst = (vbuf2, dbuf2)[arr].at[c if mine else 1 - c]
        return remote(src, dst, pair_send.at[which, arr], pair_recv.at[which, arr], partner)

    def pot_copy():
        return remote(pot, potbuf.at[1], pot_sem.at[0], pot_sem.at[1], across)

    def send_piece(k):
        for arr in range(2):
            for core in range(2):
                slab_copy(core, arr, k, True).start()

    def rows_of(k):
        if k < CHUNKS:
            return pl.ds(k * part, part)
        return pl.ds(CHUNKS * part, rows - CHUNKS * part)

    def near_copy(sems, src_e, k, dev, own=False):
        src = coeffs.at[rows_of(k)] if own else near.at[src_e, rows_of(k)]
        return remote(src, near.at[src_e, rows_of(k)], sems.at[src_e, k], near_recv.at[src_e, k], dev)

    def to_right(src_e, k, act, own=False):
        @pl.when(z < depth - 1)
        def _():
            act(near_copy(right_send, src_e, k, right, own))

    def to_left(src_e, k, act, own=False):
        @pl.when(z > 0)
        def _():
            act(near_copy(left_send, src_e, k, left, own))

    def start(copy):
        copy.start()

    def wait_send(copy):
        copy.wait_send()

    n_hop = hop.shape[0]

    def hop_pair(mine):
        return remote(
            hop, hop_all.at[:, g if mine else 2 * x + 1 - c], hop_send.at[0], hop_recv.at[0], partner
        )

    def hop_across(k, mine):
        return remote(
            hop.at[k], hop_all.at[k, g if mine else 2 * (1 - x) + c],
            hop_send.at[1 + k], hop_recv.at[1 + k], across,
        )

    def hop_relay(k, mine):
        row = 2 * (1 - x) + (c if mine else 1 - c)
        ref = hop_all.at[k, row]
        return remote(ref, ref, hop_send.at[1 + n_hop + k], hop_recv.at[1 + n_hop + k], partner)

    pot_copy().start()
    for k in range(n_hop):
        hop_across(k, True).start()
    near_copy(y_send, e, CHUNKS, y_dev, True).start()
    for k in range(CHUNKS + 1):
        to_right(e, k, start, True)
        to_left(e, k, start, True)
        if k < CHUNKS:
            near_copy(y_send, e, k, y_dev, True).start()

    loads = []

    def load(src, dst):
        copy = pltpu.make_async_copy(src, dst, load_sem.at[len(loads)])
        copy.start()
        loads.append(copy)

    for arr in range(2):
        for which in range(2):
            pair_copy(which, arr, True).start()
    for arr in range(2):
        ref = (values, derivs)[arr]
        load(ref.at[:, points(g, 0, slab)], (vbuf, dbuf)[arr].at[g])
        load(ref.at[:, points(other_slab, 0, slab)], (vbuf2, dbuf2)[arr].at[c])
    load(pot, potbuf.at[0])
    load(coeffs, near.at[e])
    load(hop, hop_all.at[:, g])
    hop_pair(True).start()
    send_piece(0)
    acc[...] = jnp.zeros_like(acc)

    def product(v_low, d_low, v_high, d_high, weight):
        weighted = (weight * v_high.astype(jnp.float32)).astype(jnp.bfloat16)
        out = 0.5 * lax.dot_general(d_low, d_high, NT, preferred_element_type=jnp.float32)
        return out + lax.dot_general(v_low, weighted, NT, preferred_element_type=jnp.float32)

    half = 2 * n_rows

    def two(ref, first, cols):
        return ref[pl.ds(first, 2), :, cols].reshape(half, piece)

    def diag_product():
        for copy in loads[:5]:
            copy.wait()
        for arr in range(2):
            for which in range(2):
                pair_copy(which, arr, False).wait_recv()
        pot_copy().wait_recv()
        acc_d[...] = jnp.zeros_like(acc_d)

        @pl.loop(0, PIECES)
        def _(k):
            cols = pl.ds(pl.multiple_of(k * piece, 128), piece)
            for vb, db, first, which in ((vbuf, dbuf, 2 * x, 0), (vbuf2, dbuf2, 0, 1)):
                v = two(vb, first, cols)
                d = two(db, first, cols)
                acc_d[...] += product(v, d, v, d, potbuf[which, :, cols]).reshape(acc_d.shape)

        remote(acc_d.at[1 - c], got_d, red_send.at[0], red_recv.at[0], partner).start()

    def diag_block(row):
        cols = pl.ds(pl.multiple_of(row // 2 * half, 128), half)
        return amat.at[pl.ds(pl.multiple_of(row * n_rows, 16), n_rows), cols]

    def diag_copy(row, which, dev):
        ref = diag_block(row)
        return remote(ref, ref, diag_send.at[which], diag_recv.at[which], dev)

    def diag_finish():
        remote(acc_d.at[1 - c], got_d, red_send.at[0], red_recv.at[0], partner).wait_recv()
        diag_block(g)[...] = (acc_d[c] + got_d[...]).astype(jnp.bfloat16)
        diag_copy(g, 0, partner).start()
        diag_copy(g, 1, across).start()

    def diag_relay(mine):
        return diag_copy(2 * (1 - x) + (c if mine else 1 - c), 2, partner)

    def diag_forward():
        diag_copy(2 * (1 - x) + c, 1, across).wait_recv()
        diag_relay(True).start()

    def off_copy(row):
        ref = amat.at[pl.ds(pl.multiple_of(row * n_rows, 16), n_rows), pl.ds(half, half)]
        return remote(ref, ref, off_send, off_recv, partner)

    def off_piece(k):
        for arr in range(2):
            for core in range(2):
                slab_copy(core, arr, k, False).wait_recv()
        cols = pl.ds(k * piece, piece)
        term = product(
            two(vbuf, 0, cols), two(dbuf, 0, cols), two(vbuf, 2, cols), two(dbuf, 2, cols),
            potbuf[0, :, cols],
        ).reshape(acc_o.shape)
        if k == 0:
            acc_o[...] = term
        else:
            acc_o[...] += term
        if k == PIECES - 1:
            remote(acc_o.at[1 - c], got_o, red_send.at[1], red_recv.at[1], partner).start()

    def off_sum():
        remote(acc_o.at[1 - c], got_o, red_send.at[1], red_recv.at[1], partner).wait_recv()
        sum_o[...] = acc_o[c] + got_o[...]
        low_o[...] = sum_o[...].astype(jnp.bfloat16)
        remote(low_o, got_x, red_send.at[2], red_recv.at[2], across).start()

    def off_finish():
        remote(low_o, got_x, red_send.at[2], red_recv.at[2], across).wait_recv()
        block = pl.ds(pl.multiple_of(c * n_rows, 16), n_rows)
        total = sum_o[...] + got_x[...].astype(jnp.float32)
        amat[block, pl.ds(half, half)] = total.astype(jnp.bfloat16)
        off_copy(c).start()

    def hop_forward(k):
        hop_across(k, False).wait_recv()
        hop_relay(k, True).start()

    def hop_ready():
        hop_pair(False).wait_recv()
        for k in range(n_hop):
            hop_relay(k, False).wait_recv()
        loads[5].wait()
        loads[6].wait()

    tile = 256

    def apply(left_of, src_e, live):
        @pl.loop(0, width // tile)
        def _(n):
            cols = pl.ds(pl.multiple_of(n * tile, tile), tile)
            ids = lax.broadcasted_iota(jnp.int32, (rows, tile), 0)
            block = near[src_e, :, cols]
            masked = jnp.where(ids < live, block, jnp.zeros_like(block))
            acc[:, cols] += jnp.dot(left_of(), masked, preferred_element_type=jnp.float32)

    def apply_hop(src_e):
        which, live = 0, 0
        for k in range(n_hop):
            same = neighbours[e, k] == src_e
            which = jnp.where(same, k, which)
            live = jnp.where(same, counts[src_e], live)
        apply(lambda: hop_all[which].reshape(rows, rows), src_e, live)

    def apply_column(d, own):
        @pl.loop(0, 2 if d else 1)
        def _(i):
            shift = d * (1 - 2 * i)
            src_e = 2 * (z + shift) + (y if own else 1 - y)

            @pl.when((z + shift >= 0) & (z + shift < depth))
            def _():
                if not own:
                    for k in range(CHUNKS):
                        near_copy(y_send, src_e, k, y_dev).wait_recv()
                apply_hop(src_e)

    def apply_own():
        diag_copy(2 * x + 1 - c, 0, partner).wait_recv()
        diag_relay(False).wait_recv()
        off_copy(1 - c).wait_recv()
        amat[pl.ds(half, half), pl.ds(0, half)] = amat[pl.ds(0, half), pl.ds(half, half)].T
        apply(lambda: amat[...], e, counts[e])

    do = functools.partial
    plan = {
        (1, 0): [diag_product],
        (1, 1): [diag_finish, do(hop_forward, 0)],
        (1, 2): [do(hop_forward, 1)],
        (1, 3): [do(hop_forward, 2), do(send_piece, 1)],
        (1, 5): [do(hop_forward, 3), diag_forward, do(send_piece, 2)],
        (2, 1): [do(off_piece, 0), do(send_piece, 3)],
        (2, 2): [hop_ready, do(apply_column, 0, False), do(apply_column, 1, True)],
        (2, 4): [do(off_piece, 1)],
        (3, 0): [do(off_piece, 2), do(apply_column, 1, False)],
        (3, 2): [do(apply_column, 2, True)],
        (3, 3): [do(off_piece, 3)],
        (3, 4): [off_sum],
        (3, 5): [off_finish, do(apply_column, 2, False)],
    }

    nbr = 2 * z + 1 - y
    near_copy(y_send, nbr, CHUNKS, y_dev).wait_recv()
    to_right(nbr, CHUNKS, start)
    to_left(nbr, CHUNKS, start)

    for d in range(1, depth):
        for k in range(CHUNKS):
            @pl.when(z >= d)
            def _():
                near_copy(right_send, e - 2 * d, k, right).wait_recv()
                to_right(e - 2 * d, k, start)
                near_copy(y_send, e - 2 * d, k, y_dev).start()

            @pl.when(z + d < depth)
            def _():
                near_copy(left_send, e + 2 * d, k, left).wait_recv()
                to_left(e + 2 * d, k, start)
                near_copy(y_send, e + 2 * d, k, y_dev).start()

            for step in plan.get((d, k), ()):
                step()
        for base in (e, nbr):
            @pl.when(z >= d)
            def _():
                near_copy(right_send, base - 2 * d, CHUNKS, right).wait_recv()
                to_right(base - 2 * d, CHUNKS, start)

            @pl.when(z + d < depth)
            def _():
                near_copy(left_send, base + 2 * d, CHUNKS, left).wait_recv()
                to_left(base + 2 * d, CHUNKS, start)

    apply_column(3, True)
    apply_own()
    apply_column(3, False)

    copies = []
    for t in range(rows // tile):
        here = pl.ds(t * tile, tile)
        ids = lax.broadcasted_iota(jnp.int32, (tile, width), 0) + t * tile
        acc[here, :] = jnp.where(ids < counts[e], acc[here, :], 0.0)
        copies.append(pltpu.make_async_copy(acc.at[here], out.at[here], out_sem.at[t]))
        copies[-1].start()

    for copy in copies:
        copy.wait()
    pot_copy().wait_send()
    for arr in range(2):
        for which in range(2):
            pair_copy(which, arr, True).wait_send()
        for core in range(2):
            for k in range(PIECES):
                slab_copy(core, arr, k, True).wait_send()
    hop_pair(True).wait_send()
    for k in range(n_hop):
        hop_across(k, True).wait_send()
        hop_relay(k, True).wait_send()
    remote(acc_d.at[1 - c], got_d, red_send.at[0], red_recv.at[0], partner).wait_send()
    remote(acc_o.at[1 - c], got_o, red_send.at[1], red_recv.at[1], partner).wait_send()
    remote(low_o, got_x, red_send.at[2], red_recv.at[2], across).wait_send()
    diag_copy(g, 0, partner).wait_send()
    diag_copy(g, 1, across).wait_send()
    diag_relay(True).wait_send()
    off_copy(c).wait_send()
    near_copy(y_send, e, CHUNKS, y_dev).wait_send()

    @pl.loop(0, depth)
    def _(zz):
        src = 2 * zz + y
        for k in range(CHUNKS):
            near_copy(y_send, src, k, y_dev).wait_send()

        @pl.when(zz <= z)
        def _():
            for k in range(CHUNKS + 1):
                to_right(src, k, wait_send)
            to_right(2 * zz + 1 - y, CHUNKS, wait_send)

        @pl.when(zz >= z)
        def _():
            for k in range(CHUNKS + 1):
                to_left(src, k, wait_send)
            to_left(2 * zz + 1 - y, CHUNKS, wait_send)


def local_kernels(basis_values, basis_derivs, potential, hop_blocks, coeffs, counts, neighbours):
    n_elem = counts.shape[0]
    width, bands = coeffs.shape[1:]
    n_rows, n_points = basis_values.shape[1:]
    slab = potential.shape[1]
    n_hop = hop_blocks.shape[1]
    n_grp = width // n_rows
    half = 2 * n_rows
    bf16, f32 = jnp.bfloat16, jnp.float32
    anywhere = pl.BlockSpec(memory_space=pl.ANY)
    dma = pltpu.SemaphoreType.DMA
    vmem = pltpu.VMEM
    flops = 2 * half * half * 3 * 2 * slab
    smem = pl.BlockSpec(memory_space=pltpu.SMEM)
    out = pl.pallas_call(
        hamiltonian_kernel,
        out_shape=jax.ShapeDtypeStruct((width, bands), f32),
        in_specs=[anywhere] * 5 + [smem] * 2,
        out_specs=anywhere,
        scratch_shapes=[
            vmem((n_elem, width, bands), bf16), vmem((n_hop, n_grp, n_rows, width), bf16),
            vmem((width, width), bf16), vmem((width, bands), f32),
            vmem((n_grp, n_rows, slab), bf16), vmem((n_grp, n_rows, slab), bf16),
            vmem((2, n_rows, slab), bf16), vmem((2, n_rows, slab), bf16),
            vmem((2, 1, slab), f32),
            vmem((2, n_rows, half), f32), vmem((2, n_rows, half), f32),
            vmem((n_rows, half), f32), vmem((n_rows, half), f32), vmem((n_rows, half), f32),
            vmem((n_rows, half), bf16), vmem((n_rows, half), bf16),
            dma((7,)), dma((2, 2)), dma((2, 2)), dma((2, 2, PIECES)), dma((2, 2, PIECES)), dma((2,)),
            dma((3,)), dma((3,)), dma((3,)), dma((3,)), dma, dma,
            dma((1 + 2 * n_hop,)), dma((1 + 2 * n_hop,)),
            dma((n_elem, CHUNKS + 1)), dma((n_elem, CHUNKS + 1)),
            dma((n_elem, CHUNKS + 1)), dma((n_elem, CHUNKS + 1)), dma((4,)),
        ],
        compiler_params=pltpu.CompilerParams(
            collective_id=0, has_side_effects=True, vmem_limit_bytes=60 * 2 ** 20
        ),
        cost_estimate=pl.CostEstimate(
            flops=flops + 2 * n_elem * width * width * bands, bytes_accessed=2 ** 25, transcendentals=0
        ),
        name="hamiltonian",
    )(
        basis_values[0], basis_derivs[0], potential, hop_blocks[0], coeffs[0], counts, neighbours
    )
    return out[None]


def solution(mesh):
    placed = (
        P("elem", "grp", None),
        P("elem", "grp", None),
        P("elem", "grp"),
        P("elem", None, "grp", None),
        P("elem", None, "grp"),
        P(),
        P(),
    )
    fits = mesh.shape["elem"] == 8 and mesh.shape["grp"] == 4
    return jax.shard_map(
        local_kernels if fits else local,
        mesh=mesh, in_specs=placed, out_specs=P("elem", None, "grp"), check_vma=False,
    )
```

```python
import functools

import jax
import jax.numpy as jnp
from jax import lax
from jax.experimental import pallas as pl
from jax.experimental.pallas import tpu as pltpu
from jax.sharding import PartitionSpec as P


def local(basis_values, basis_derivs, potential, hop_blocks, coeffs, counts, neighbours):
    values_slab, derivs_slab = (
        lax.all_to_all(basis_values, "grp", split_axis=2, concat_axis=1, tiled=True),
        lax.all_to_all(basis_derivs, "grp", split_axis=2, concat_axis=1, tiled=True),
    )
    values_slab = values_slab[0]
    derivs_slab = derivs_slab[0]
    weighted = (potential[0][None, :] * values_slab.astype(jnp.float32)).astype(jnp.bfloat16)
    partial_value = 0.5 * jnp.einsum(
        "ip,jp->ij", derivs_slab, derivs_slab, preferred_element_type=jnp.float32
    )
    partial_value = partial_value + jnp.einsum(
        "ip,jp->ij", values_slab, weighted, preferred_element_type=jnp.float32
    )
    element = lax.axis_index("elem")
    width = coeffs.shape[1]
    row_ids = jnp.arange(width, dtype=jnp.int32)
    live_rows = row_ids < counts[element]
    own_coeffs = jnp.where(live_rows[:, None], coeffs[0], jnp.zeros_like(coeffs[0]))
    near_ids = neighbours[element]
    initial = jnp.zeros((near_ids.shape[0], width, coeffs.shape[2]), jnp.bfloat16)
    pieces = lax.all_gather(own_coeffs[None], "elem", axis=0, tiled=True)
    inside = (near_ids >= 0) & (near_ids < pieces.shape[0])
    clipped = jnp.clip(near_ids, 0, pieces.shape[0] - 1)
    picked = jnp.take(pieces, clipped, axis=0)
    near_coeffs = jnp.where(inside[:, None, None], picked, initial)
    assembled_low = lax.psum(partial_value, "grp").astype(jnp.bfloat16)
    applied = jnp.dot(assembled_low, own_coeffs, preferred_element_type=jnp.float32)
    applied = applied + jnp.einsum(
        "krm,kmb->rb",
        lax.all_gather(hop_blocks, "grp", axis=2, tiled=True)[0],
        near_coeffs,
        preferred_element_type=jnp.float32,
    )
    result = jnp.where(live_rows[:, None], applied, jnp.zeros_like(applied))
    return result[None]


NT = (((1,), (1,)), ((), ()))
PIECES = 4
CHUNKS = 6


def hamiltonian_kernel(
    values, derivs, pot, hop, coeffs, counts, neighbours, out, a_out,
    near, hop_all, amat, acc,
    vbuf, dbuf, vbuf2, dbuf2, potbuf, acc_d, acc_o, got_d, got_o, sum_o, low_o, got_x,
    load_sem, pair_send, pair_recv, slab_send, slab_recv, pot_sem, red_send, red_recv,
    diag_send, diag_recv, off_send, off_recv, hop_send, hop_recv,
    right_send, left_send, y_send, near_recv, out_sem,
):
    e = lax.axis_index("elem")
    g = lax.axis_index("grp")
    z, y = e // 2, e % 2
    x, c = g // 2, g % 2
    partner = {"grp": 2 * x + 1 - c}
    across = {"grp": 2 * (1 - x) + c}
    beyond = {"grp": 2 * (1 - x) + 1 - c}
    y_dev = {"elem": 2 * z + 1 - y}
    right = {"elem": e + 2}
    left = {"elem": e - 2}
    depth = 4
    rows, width = coeffs.shape
    part = rows * 9 // 64 // 16 * 16
    n_rows, slab = vbuf.shape[1], vbuf.shape[2]
    piece = slab // PIECES
    other_slab = 2 * (1 - x) + c

    def remote(src, dst, ss, rs, dev):
        return pltpu.make_async_remote_copy(
            src_ref=src, dst_ref=dst, send_sem=ss, recv_sem=rs,
            device_id=dev, device_id_type=pl.DeviceIdType.MESH,
        )

    barrier = pltpu.get_barrier_semaphore()
    for dev in (partner, across, beyond, y_dev):
        pl.semaphore_signal(barrier, inc=1, device_id=dev, device_id_type=pl.DeviceIdType.MESH)

    @pl.when(z < depth - 1)
    def _():
        pl.semaphore_signal(barrier, inc=1, device_id=right, device_id_type=pl.DeviceIdType.MESH)

    @pl.when(z > 0)
    def _():
        pl.semaphore_signal(barrier, inc=1, device_id=left, device_id_type=pl.DeviceIdType.MESH)

    pl.semaphore_wait(barrier, 4 + (z + depth - 2) // (depth - 1) + (2 * depth - 3 - z) // (depth - 1))

    def points(which, start, size):
        return pl.ds(pl.multiple_of(which * slab + start, 128), size)

    def slab_copy(core, arr, k, mine):
        src = (values, derivs)[arr].at[:, points(2 * (1 - x) + core, k * piece, piece)]
        row = g if mine else 2 * (1 - x) + core
        dst = (vbuf, dbuf)[arr].at[row, :, pl.ds(k * piece, piece)]
        return remote(
            src, dst, slab_send.at[core, arr, k],
            slab_recv.at[c if mine else core, arr, k], {"grp": 2 * (1 - x) + core},
        )

    def pair_copy(which, arr, mine):
        ref = (values, derivs)[arr]
        their = 1 - c if mine else c
        src = ref.at[:, points(2 * x + their if which == 0 else 2 * (1 - x) + their, 0, slab)]
        if which == 0:
            dst = (vbuf, dbuf)[arr].at[g if mine else 2 * x + 1 - c]
        else:
            dst = (vbuf2, dbuf2)[arr].at[c if mine else 1 - c]
        return remote(src, dst, pair_send.at[which, arr], pair_recv.at[which, arr], partner)

    def pot_copy():
        return remote(pot, potbuf.at[1], pot_sem.at[0], pot_sem.at[1], across)

    def send_piece(k):
        for arr in range(2):
            for core in range(2):
                slab_copy(core, arr, k, True).start()

    first = CHUNKS * part - 16

    def rows_of(k):
        if k < CHUNKS - 1:
            return pl.ds(k * part, part)
        if k == CHUNKS - 1:
            return pl.ds(k * part, first - k * part)
        return pl.ds(first, rows - first)

    def near_copy(sems, src_e, k, dev, own=False):
        src = coeffs.at[rows_of(k)] if own else near.at[src_e, rows_of(k)]
        return remote(src, near.at[src_e, rows_of(k)], sems.at[src_e, k], near_recv.at[src_e, k], dev)

    def to_right(src_e, k, act, own=False):
        @pl.when(z < depth - 1)
        def _():
            act(near_copy(right_send, src_e, k, right, own))

    def to_left(src_e, k, act, own=False):
        @pl.when(z > 0)
        def _():
            act(near_copy(left_send, src_e, k, left, own))

    def start(copy):
        copy.start()

    def wait_send(copy):
        copy.wait_send()

    n_hop = hop.shape[0]

    def hop_pair(mine):
        return remote(
            hop, hop_all.at[:, g if mine else 2 * x + 1 - c], hop_send.at[0], hop_recv.at[0], partner
        )

    def hop_across(k, mine):
        return remote(
            hop.at[k], hop_all.at[k, g if mine else 2 * (1 - x) + c],
            hop_send.at[1 + k], hop_recv.at[1 + k], across,
        )

    def hop_relay(k, mine):
        row = 2 * (1 - x) + (c if mine else 1 - c)
        ref = hop_all.at[k, row]
        return remote(ref, ref, hop_send.at[1 + n_hop + k], hop_recv.at[1 + n_hop + k], partner)

    pot_copy().start()
    for k in range(n_hop):
        hop_across(k, True).start()
    near_copy(y_send, e, CHUNKS, y_dev, True).start()
    for k in range(CHUNKS + 1):
        to_right(e, k, start, True)
        to_left(e, k, start, True)
        if k < CHUNKS:
            near_copy(y_send, e, k, y_dev, True).start()

    loads = []

    def load(src, dst):
        copy = pltpu.make_async_copy(src, dst, load_sem.at[len(loads)])
        copy.start()
        loads.append(copy)

    for arr in range(2):
        for which in range(2):
            pair_copy(which, arr, True).start()
    for arr in range(2):
        ref = (values, derivs)[arr]
        load(ref.at[:, points(g, 0, slab)], (vbuf, dbuf)[arr].at[g])
        load(ref.at[:, points(other_slab, 0, slab)], (vbuf2, dbuf2)[arr].at[c])
    load(pot, potbuf.at[0])
    load(coeffs, near.at[e])
    load(hop, hop_all.at[:, g])
    hop_pair(True).start()
    send_piece(0)
    acc[...] = jnp.zeros_like(acc)

    def product(v_low, d_low, v_high, d_high, weight):
        weighted = (weight * v_high.astype(jnp.float32)).astype(jnp.bfloat16)
        out = 0.5 * lax.dot_general(d_low, d_high, NT, preferred_element_type=jnp.float32)
        return out + lax.dot_general(v_low, weighted, NT, preferred_element_type=jnp.float32)

    half = 2 * n_rows

    def two(ref, first, cols):
        return ref[pl.ds(first, 2), :, cols].reshape(half, piece)

    def diag_product():
        for copy in loads[:5]:
            copy.wait()
        for arr in range(2):
            for which in range(2):
                pair_copy(which, arr, False).wait_recv()
        pot_copy().wait_recv()
        acc_d[...] = jnp.zeros_like(acc_d)

        @pl.loop(0, PIECES)
        def _(k):
            cols = pl.ds(pl.multiple_of(k * piece, 128), piece)
            for vb, db, first, which in ((vbuf, dbuf, 2 * x, 0), (vbuf2, dbuf2, 0, 1)):
                v = two(vb, first, cols)
                d = two(db, first, cols)
                acc_d[...] += product(v, d, v, d, potbuf[which, :, cols]).reshape(acc_d.shape)

        remote(acc_d.at[1 - c], got_d, red_send.at[0], red_recv.at[0], partner).start()

    def diag_block(row):
        cols = pl.ds(pl.multiple_of(row // 2 * half, 128), half)
        return amat.at[pl.ds(pl.multiple_of(row * n_rows, 16), n_rows), cols]

    def diag_copy(row, which, dev):
        ref = diag_block(row)
        return remote(ref, ref, diag_send.at[which], diag_recv.at[which], dev)

    def diag_finish():
        remote(acc_d.at[1 - c], got_d, red_send.at[0], red_recv.at[0], partner).wait_recv()
        diag_block(g)[...] = (acc_d[c] + got_d[...]).astype(jnp.bfloat16)
        diag_copy(g, 0, partner).start()
        diag_copy(g, 1, across).start()

    def diag_relay(mine):
        return diag_copy(2 * (1 - x) + (c if mine else 1 - c), 2, partner)

    def diag_forward():
        diag_copy(2 * (1 - x) + c, 1, across).wait_recv()
        diag_relay(True).start()

    def off_copy(row):
        ref = amat.at[pl.ds(pl.multiple_of(row * n_rows, 16), n_rows), pl.ds(half, half)]
        return remote(ref, ref, off_send, off_recv, partner)

    def off_piece(k):
        for arr in range(2):
            for core in range(2):
                slab_copy(core, arr, k, False).wait_recv()
        cols = pl.ds(k * piece, piece)
        term = product(
            two(vbuf, 0, cols), two(dbuf, 0, cols), two(vbuf, 2, cols), two(dbuf, 2, cols),
            potbuf[0, :, cols],
        ).reshape(acc_o.shape)
        if k == 0:
            acc_o[...] = term
        else:
            acc_o[...] += term
        if k == PIECES - 1:
            remote(acc_o.at[1 - c], got_o, red_send.at[1], red_recv.at[1], partner).start()

    def off_sum():
        remote(acc_o.at[1 - c], got_o, red_send.at[1], red_recv.at[1], partner).wait_recv()
        sum_o[...] = acc_o[c] + got_o[...]
        low_o[...] = sum_o[...].astype(jnp.bfloat16)
        remote(low_o, got_x, red_send.at[2], red_recv.at[2], across).start()

    def off_finish():
        remote(low_o, got_x, red_send.at[2], red_recv.at[2], across).wait_recv()
        block = pl.ds(pl.multiple_of(c * n_rows, 16), n_rows)
        total = sum_o[...] + got_x[...].astype(jnp.float32)
        amat[block, pl.ds(half, half)] = total.astype(jnp.bfloat16)
        off_copy(c).start()

    def hop_forward(k):
        hop_across(k, False).wait_recv()
        hop_relay(k, True).start()

    def hop_ready():
        hop_pair(False).wait_recv()
        for k in range(n_hop):
            hop_relay(k, False).wait_recv()
        loads[5].wait()
        loads[6].wait()

    tile = 256
    copies = []

    def apply(left_of, src_e, live):
        @pl.loop(0, width // tile)
        def _(n):
            cols = pl.ds(pl.multiple_of(n * tile, tile), tile)
            ids = lax.broadcasted_iota(jnp.int32, (rows, tile), 0)
            block = near[src_e, :, cols]
            masked = jnp.where(ids < live, block, jnp.zeros_like(block))
            acc[:, cols] += jnp.dot(left_of(), masked, preferred_element_type=jnp.float32)

    def apply_hop(src_e):
        which, live = 0, 0
        for k in range(n_hop):
            same = neighbours[k, e] == src_e
            which = jnp.where(same, k, which)
            live = jnp.where(same, counts[src_e], live)
        apply(lambda: hop_all[which].reshape(rows, rows), src_e, live)

    def apply_column(d, own):
        @pl.loop(0, 2 if d else 1)
        def _(i):
            shift = d * (1 - 2 * i)
            src_e = 2 * (z + shift) + (y if own else 1 - y)

            @pl.when((z + shift >= 0) & (z + shift < depth))
            def _():
                if not own:
                    for k in range(CHUNKS):
                        near_copy(y_send, src_e, k, y_dev).wait_recv()
                apply_hop(src_e)

    def finish_own():
        diag_copy(2 * x + 1 - c, 0, partner).wait_recv()
        diag_relay(False).wait_recv()
        off_copy(1 - c).wait_recv()
        amat[pl.ds(half, half), pl.ds(0, half)] = amat[pl.ds(0, half), pl.ds(half, half)].T
        copies.append(pltpu.make_async_copy(amat, a_out, out_sem.at[0]))
        copies[-1].start()

    do = functools.partial
    plan = {
        (1, 0): [diag_product],
        (1, 1): [diag_finish, do(hop_forward, 0)],
        (1, 2): [do(hop_forward, 1)],
        (1, 3): [do(hop_forward, 2), do(send_piece, 1)],
        (1, 5): [do(hop_forward, 3), diag_forward, do(send_piece, 2)],
        (2, 1): [do(off_piece, 0), do(send_piece, 3)],
        (2, 2): [hop_ready, do(apply_column, 0, False), do(apply_column, 1, True)],
        (2, 4): [do(off_piece, 1)],
        (3, 0): [do(off_piece, 2), do(apply_column, 1, False)],
        (3, 2): [do(apply_column, 2, True)],
        (3, 3): [do(off_piece, 3)],
        (3, 4): [off_sum],
        (3, 5): [off_finish, do(apply_column, 2, False)],
    }

    nbr = 2 * z + 1 - y
    near_copy(y_send, nbr, CHUNKS, y_dev).wait_recv()
    to_right(nbr, CHUNKS, start)
    to_left(nbr, CHUNKS, start)

    for d in range(1, depth):
        for k in range(CHUNKS):
            @pl.when(z >= d)
            def _():
                near_copy(right_send, e - 2 * d, k, right).wait_recv()
                to_right(e - 2 * d, k, start)
                near_copy(y_send, e - 2 * d, k, y_dev).start()

            @pl.when(z + d < depth)
            def _():
                near_copy(left_send, e + 2 * d, k, left).wait_recv()
                to_left(e + 2 * d, k, start)
                near_copy(y_send, e + 2 * d, k, y_dev).start()

            for step in plan.get((d, k), ()):
                step()
        for base in (e, nbr):
            @pl.when(z >= d)
            def _():
                near_copy(right_send, base - 2 * d, CHUNKS, right).wait_recv()
                to_right(base - 2 * d, CHUNKS, start)

            @pl.when(z + d < depth)
            def _():
                near_copy(left_send, base + 2 * d, CHUNKS, left).wait_recv()
                to_left(base + 2 * d, CHUNKS, start)

    apply_column(3, True)
    finish_own()
    apply_column(3, False)

    copies.append(pltpu.make_async_copy(acc, out, out_sem.at[1]))
    copies[-1].start()

    for copy in copies:
        copy.wait()
    pot_copy().wait_send()
    for arr in range(2):
        for which in range(2):
            pair_copy(which, arr, True).wait_send()
        for core in range(2):
            for k in range(PIECES):
                slab_copy(core, arr, k, True).wait_send()
    hop_pair(True).wait_send()
    for k in range(n_hop):
        hop_across(k, True).wait_send()
        hop_relay(k, True).wait_send()
    remote(acc_d.at[1 - c], got_d, red_send.at[0], red_recv.at[0], partner).wait_send()
    remote(acc_o.at[1 - c], got_o, red_send.at[1], red_recv.at[1], partner).wait_send()
    remote(low_o, got_x, red_send.at[2], red_recv.at[2], across).wait_send()
    diag_copy(g, 0, partner).wait_send()
    diag_copy(g, 1, across).wait_send()
    diag_relay(True).wait_send()
    off_copy(c).wait_send()
    near_copy(y_send, e, CHUNKS, y_dev).wait_send()

    @pl.loop(0, depth)
    def _(zz):
        src = 2 * zz + y
        for k in range(CHUNKS):
            near_copy(y_send, src, k, y_dev).wait_send()

        @pl.when(zz <= z)
        def _():
            for k in range(CHUNKS + 1):
                to_right(src, k, wait_send)
            to_right(2 * zz + 1 - y, CHUNKS, wait_send)

        @pl.when(zz >= z)
        def _():
            for k in range(CHUNKS + 1):
                to_left(src, k, wait_send)
            to_left(2 * zz + 1 - y, CHUNKS, wait_send)


def own_kernel(counts, assembled, coeffs, hops, out):
    live = counts[lax.axis_index("elem")]
    ids = lax.broadcasted_iota(jnp.int32, coeffs.shape, 0)
    masked = jnp.where(ids < live, coeffs[...], jnp.zeros_like(coeffs))
    total = hops[...] + jnp.dot(assembled[...], masked, preferred_element_type=jnp.float32)
    ids = lax.broadcasted_iota(jnp.int32, out.shape, 0)
    out[...] = jnp.where(ids < live, total, 0.0)


def local_kernels(basis_values, basis_derivs, potential, hop_blocks, coeffs, counts, neighbours):
    n_elem = counts.shape[0]
    width, bands = coeffs.shape[1:]
    n_rows, n_points = basis_values.shape[1:]
    slab = potential.shape[1]
    n_hop = hop_blocks.shape[1]
    n_grp = width // n_rows
    half = 2 * n_rows
    bf16, f32 = jnp.bfloat16, jnp.float32
    anywhere = pl.BlockSpec(memory_space=pl.ANY)
    dma = pltpu.SemaphoreType.DMA
    vmem = pltpu.VMEM
    flops = 2 * half * half * 3 * 2 * slab
    smem = pl.BlockSpec(memory_space=pltpu.SMEM)
    hops, assembled = pl.pallas_call(
        hamiltonian_kernel,
        out_shape=(
            jax.ShapeDtypeStruct((width, bands), f32), jax.ShapeDtypeStruct((width, width), bf16),
        ),
        in_specs=[anywhere] * 5 + [smem] * 2,
        out_specs=(anywhere, anywhere),
        scratch_shapes=[
            vmem((n_elem, width, bands), bf16), vmem((n_hop, n_grp, n_rows, width), bf16),
            vmem((width, width), bf16), vmem((width, bands), f32),
            vmem((n_grp, n_rows, slab), bf16), vmem((n_grp, n_rows, slab), bf16),
            vmem((2, n_rows, slab), bf16), vmem((2, n_rows, slab), bf16),
            vmem((2, 1, slab), f32),
            vmem((2, n_rows, half), f32), vmem((2, n_rows, half), f32),
            vmem((n_rows, half), f32), vmem((n_rows, half), f32), vmem((n_rows, half), f32),
            vmem((n_rows, half), bf16), vmem((n_rows, half), bf16),
            dma((7,)), dma((2, 2)), dma((2, 2)), dma((2, 2, PIECES)), dma((2, 2, PIECES)), dma((2,)),
            dma((3,)), dma((3,)), dma((3,)), dma((3,)), dma, dma,
            dma((1 + 2 * n_hop,)), dma((1 + 2 * n_hop,)),
            dma((n_elem, CHUNKS + 1)), dma((n_elem, CHUNKS + 1)),
            dma((n_elem, CHUNKS + 1)), dma((n_elem, CHUNKS + 1)), dma((2,)),
        ],
        compiler_params=pltpu.CompilerParams(
            collective_id=0, has_side_effects=True, vmem_limit_bytes=60 * 2 ** 20
        ),
        cost_estimate=pl.CostEstimate(
            flops=flops + 2 * n_elem * width * width * bands, bytes_accessed=2 ** 25, transcendentals=0
        ),
        name="hamiltonian",
    )(
        basis_values[0], basis_derivs[0], potential, hop_blocks[0], coeffs[0], counts, neighbours.T
    )
    tile = 256
    column = pl.BlockSpec((width, tile), lambda n: (0, n))
    out = pl.pallas_call(
        own_kernel,
        out_shape=jax.ShapeDtypeStruct((width, bands), f32),
        grid=(bands // tile,),
        in_specs=[smem, pl.BlockSpec((width, width), lambda n: (0, 0)), column, column],
        out_specs=column,
        compiler_params=pltpu.CompilerParams(vmem_limit_bytes=60 * 2 ** 20),
        cost_estimate=pl.CostEstimate(
            flops=2 * width * width * bands, bytes_accessed=2 ** 24, transcendentals=0
        ),
        name="own",
    )(counts, assembled, coeffs[0], hops)
    return out[None]


def solution(mesh):
    placed = (
        P("elem", "grp", None),
        P("elem", "grp", None),
        P("elem", "grp"),
        P("elem", None, "grp", None),
        P("elem", None, "grp"),
        P(),
        P(),
    )
    fits = mesh.shape["elem"] == 8 and mesh.shape["grp"] == 4
    return jax.shard_map(
        local_kernels if fits else local,
        mesh=mesh, in_specs=placed, out_specs=P("elem", None, "grp"), check_vma=False,
    )
```

```python
import functools

import jax
import jax.numpy as jnp
from jax import lax
from jax.experimental import pallas as pl
from jax.experimental.pallas import tpu as pltpu
from jax.sharding import PartitionSpec as P


def local(basis_values, basis_derivs, potential, hop_blocks, coeffs, counts, neighbours):
    values_slab, derivs_slab = (
        lax.all_to_all(basis_values, "grp", split_axis=2, concat_axis=1, tiled=True),
        lax.all_to_all(basis_derivs, "grp", split_axis=2, concat_axis=1, tiled=True),
    )
    values_slab = values_slab[0]
    derivs_slab = derivs_slab[0]
    weighted = (potential[0][None, :] * values_slab.astype(jnp.float32)).astype(jnp.bfloat16)
    partial_value = 0.5 * jnp.einsum(
        "ip,jp->ij", derivs_slab, derivs_slab, preferred_element_type=jnp.float32
    )
    partial_value = partial_value + jnp.einsum(
        "ip,jp->ij", values_slab, weighted, preferred_element_type=jnp.float32
    )
    element = lax.axis_index("elem")
    width = coeffs.shape[1]
    row_ids = jnp.arange(width, dtype=jnp.int32)
    live_rows = row_ids < counts[element]
    own_coeffs = jnp.where(live_rows[:, None], coeffs[0], jnp.zeros_like(coeffs[0]))
    near_ids = neighbours[element]
    initial = jnp.zeros((near_ids.shape[0], width, coeffs.shape[2]), jnp.bfloat16)
    pieces = lax.all_gather(own_coeffs[None], "elem", axis=0, tiled=True)
    inside = (near_ids >= 0) & (near_ids < pieces.shape[0])
    clipped = jnp.clip(near_ids, 0, pieces.shape[0] - 1)
    picked = jnp.take(pieces, clipped, axis=0)
    near_coeffs = jnp.where(inside[:, None, None], picked, initial)
    assembled_low = lax.psum(partial_value, "grp").astype(jnp.bfloat16)
    applied = jnp.dot(assembled_low, own_coeffs, preferred_element_type=jnp.float32)
    applied = applied + jnp.einsum(
        "krm,kmb->rb",
        lax.all_gather(hop_blocks, "grp", axis=2, tiled=True)[0],
        near_coeffs,
        preferred_element_type=jnp.float32,
    )
    result = jnp.where(live_rows[:, None], applied, jnp.zeros_like(applied))
    return result[None]


NT = (((1,), (1,)), ((), ()))
PIECES = 4
CHUNKS = 6


def hamiltonian_kernel(
    values, derivs, pot, hop, coeffs, counts, neighbours, out,
    near, hop_all, amat, acc,
    vbuf, dbuf, vbuf2, dbuf2, potbuf, acc_d, acc_o, got_d, got_o, sum_o, low_o, got_x,
    load_sem, pair_send, pair_recv, slab_send, slab_recv, pot_sem, red_send, red_recv,
    diag_send, diag_recv, off_send, off_recv, hop_send, hop_recv,
    right_send, left_send, y_send, near_recv, out_sem,
):
    e = lax.axis_index("elem")
    g = lax.axis_index("grp")
    z, y = e // 2, e % 2
    x, c = g // 2, g % 2
    partner = {"grp": 2 * x + 1 - c}
    across = {"grp": 2 * (1 - x) + c}
    beyond = {"grp": 2 * (1 - x) + 1 - c}
    y_dev = {"elem": 2 * z + 1 - y}
    right = {"elem": e + 2}
    left = {"elem": e - 2}
    depth = 4
    rows, width = coeffs.shape
    part = rows * 9 // 64 // 16 * 16
    n_rows, slab = vbuf.shape[1], vbuf.shape[2]
    piece = slab // PIECES
    other_slab = 2 * (1 - x) + c

    def remote(src, dst, ss, rs, dev):
        return pltpu.make_async_remote_copy(
            src_ref=src, dst_ref=dst, send_sem=ss, recv_sem=rs,
            device_id=dev, device_id_type=pl.DeviceIdType.MESH,
        )

    barrier = pltpu.get_barrier_semaphore()
    for dev in (partner, across, beyond, y_dev):
        pl.semaphore_signal(barrier, inc=1, device_id=dev, device_id_type=pl.DeviceIdType.MESH)

    @pl.when(z < depth - 1)
    def _():
        pl.semaphore_signal(barrier, inc=1, device_id=right, device_id_type=pl.DeviceIdType.MESH)

    @pl.when(z > 0)
    def _():
        pl.semaphore_signal(barrier, inc=1, device_id=left, device_id_type=pl.DeviceIdType.MESH)

    pl.semaphore_wait(barrier, 4 + (z + depth - 2) // (depth - 1) + (2 * depth - 3 - z) // (depth - 1))

    def points(which, start, size):
        return pl.ds(pl.multiple_of(which * slab + start, 128), size)

    def slab_copy(core, arr, k, mine):
        src = (values, derivs)[arr].at[:, points(2 * (1 - x) + core, k * piece, piece)]
        row = g if mine else 2 * (1 - x) + core
        dst = (vbuf, dbuf)[arr].at[row, :, pl.ds(k * piece, piece)]
        return remote(
            src, dst, slab_send.at[core, arr, k],
            slab_recv.at[c if mine else core, arr, k], {"grp": 2 * (1 - x) + core},
        )

    def pair_copy(which, arr, mine):
        ref = (values, derivs)[arr]
        their = 1 - c if mine else c
        src = ref.at[:, points(2 * x + their if which == 0 else 2 * (1 - x) + their, 0, slab)]
        if which == 0:
            dst = (vbuf, dbuf)[arr].at[g if mine else 2 * x + 1 - c]
        else:
            dst = (vbuf2, dbuf2)[arr].at[c if mine else 1 - c]
        return remote(src, dst, pair_send.at[which, arr], pair_recv.at[which, arr], partner)

    def pot_copy():
        return remote(pot, potbuf.at[1], pot_sem.at[0], pot_sem.at[1], across)

    def send_piece(k):
        for arr in range(2):
            for core in range(2):
                slab_copy(core, arr, k, True).start()

    first = CHUNKS * part - 16

    def rows_of(k):
        if k < CHUNKS - 1:
            return pl.ds(k * part, part)
        if k == CHUNKS - 1:
            return pl.ds(k * part, first - k * part)
        return pl.ds(first, rows - first)

    def near_copy(sems, src_e, k, dev, own=False):
        src = coeffs.at[rows_of(k)] if own else near.at[src_e, rows_of(k)]
        return remote(src, near.at[src_e, rows_of(k)], sems.at[src_e, k], near_recv.at[src_e, k], dev)

    def to_right(src_e, k, act, own=False):
        @pl.when(z < depth - 1)
        def _():
            act(near_copy(right_send, src_e, k, right, own))

    def to_left(src_e, k, act, own=False):
        @pl.when(z > 0)
        def _():
            act(near_copy(left_send, src_e, k, left, own))

    def start(copy):
        copy.start()

    def wait_send(copy):
        copy.wait_send()

    n_hop = hop.shape[0]

    def hop_pair(mine):
        return remote(
            hop, hop_all.at[:, g if mine else 2 * x + 1 - c], hop_send.at[0], hop_recv.at[0], partner
        )

    def hop_across(k, mine):
        return remote(
            hop.at[k], hop_all.at[k, g if mine else 2 * (1 - x) + c],
            hop_send.at[1 + k], hop_recv.at[1 + k], across,
        )

    def hop_relay(k, mine):
        row = 2 * (1 - x) + (c if mine else 1 - c)
        ref = hop_all.at[k, row]
        return remote(ref, ref, hop_send.at[1 + n_hop + k], hop_recv.at[1 + n_hop + k], partner)

    pot_copy().start()
    for k in range(n_hop):
        hop_across(k, True).start()
    near_copy(y_send, e, CHUNKS, y_dev, True).start()
    for k in range(CHUNKS + 1):
        to_right(e, k, start, True)
        to_left(e, k, start, True)
        if k < CHUNKS:
            near_copy(y_send, e, k, y_dev, True).start()

    loads = []

    def load(src, dst):
        copy = pltpu.make_async_copy(src, dst, load_sem.at[len(loads)])
        copy.start()
        loads.append(copy)

    for arr in range(2):
        for which in range(2):
            pair_copy(which, arr, True).start()
    for arr in range(2):
        ref = (values, derivs)[arr]
        load(ref.at[:, points(g, 0, slab)], (vbuf, dbuf)[arr].at[g])
        load(ref.at[:, points(other_slab, 0, slab)], (vbuf2, dbuf2)[arr].at[c])
    load(pot, potbuf.at[0])
    load(coeffs, near.at[e])
    load(hop, hop_all.at[:, g])
    hop_pair(True).start()
    send_piece(0)
    acc[...] = jnp.zeros_like(acc)

    def product(v_low, d_low, v_high, d_high, weight):
        weighted = (weight * v_high.astype(jnp.float32)).astype(jnp.bfloat16)
        out = 0.5 * lax.dot_general(d_low, d_high, NT, preferred_element_type=jnp.float32)
        return out + lax.dot_general(v_low, weighted, NT, preferred_element_type=jnp.float32)

    half = 2 * n_rows

    def two(ref, first, cols):
        return ref[pl.ds(first, 2), :, cols].reshape(half, piece)

    def diag_product():
        for copy in loads[:5]:
            copy.wait()
        for arr in range(2):
            for which in range(2):
                pair_copy(which, arr, False).wait_recv()
        pot_copy().wait_recv()
        acc_d[...] = jnp.zeros_like(acc_d)

        @pl.loop(0, PIECES)
        def _(k):
            cols = pl.ds(pl.multiple_of(k * piece, 128), piece)
            for vb, db, first, which in ((vbuf, dbuf, 2 * x, 0), (vbuf2, dbuf2, 0, 1)):
                v = two(vb, first, cols)
                d = two(db, first, cols)
                acc_d[...] += product(v, d, v, d, potbuf[which, :, cols]).reshape(acc_d.shape)

        remote(acc_d.at[1 - c], got_d, red_send.at[0], red_recv.at[0], partner).start()

    def diag_block(row):
        cols = pl.ds(pl.multiple_of(row // 2 * half, 128), half)
        return amat.at[pl.ds(pl.multiple_of(row * n_rows, 16), n_rows), cols]

    def diag_copy(row, which, dev):
        ref = diag_block(row)
        return remote(ref, ref, diag_send.at[which], diag_recv.at[which], dev)

    def diag_finish():
        remote(acc_d.at[1 - c], got_d, red_send.at[0], red_recv.at[0], partner).wait_recv()
        diag_block(g)[...] = (acc_d[c] + got_d[...]).astype(jnp.bfloat16)
        diag_copy(g, 0, partner).start()
        diag_copy(g, 1, across).start()

    def diag_relay(mine):
        return diag_copy(2 * (1 - x) + (c if mine else 1 - c), 2, partner)

    def diag_forward():
        diag_copy(2 * (1 - x) + c, 1, across).wait_recv()
        diag_relay(True).start()

    def off_copy(row):
        ref = amat.at[pl.ds(pl.multiple_of(row * n_rows, 16), n_rows), pl.ds(half, half)]
        return remote(ref, ref, off_send, off_recv, partner)

    def off_piece(k):
        for arr in range(2):
            for core in range(2):
                slab_copy(core, arr, k, False).wait_recv()
        cols = pl.ds(k * piece, piece)
        term = product(
            two(vbuf, 0, cols), two(dbuf, 0, cols), two(vbuf, 2, cols), two(dbuf, 2, cols),
            potbuf[0, :, cols],
        ).reshape(acc_o.shape)
        if k == 0:
            acc_o[...] = term
        else:
            acc_o[...] += term
        if k == PIECES - 1:
            remote(acc_o.at[1 - c], got_o, red_send.at[1], red_recv.at[1], partner).start()

    def off_sum():
        remote(acc_o.at[1 - c], got_o, red_send.at[1], red_recv.at[1], partner).wait_recv()
        sum_o[...] = acc_o[c] + got_o[...]
        low_o[...] = sum_o[...].astype(jnp.bfloat16)
        remote(low_o, got_x, red_send.at[2], red_recv.at[2], across).start()

    def off_finish():
        remote(low_o, got_x, red_send.at[2], red_recv.at[2], across).wait_recv()
        block = pl.ds(pl.multiple_of(c * n_rows, 16), n_rows)
        total = sum_o[...] + got_x[...].astype(jnp.float32)
        amat[block, pl.ds(half, half)] = total.astype(jnp.bfloat16)
        off_copy(c).start()

    def hop_forward(k):
        hop_across(k, False).wait_recv()
        hop_relay(k, True).start()

    def hop_ready():
        hop_pair(False).wait_recv()
        for k in range(n_hop):
            hop_relay(k, False).wait_recv()
        loads[5].wait()
        loads[6].wait()

    tile = 256

    def columns(n):
        return pl.ds(pl.multiple_of(n * tile, tile), tile)

    def add_product(n, left, src_e, live):
        cols = columns(n)
        ids = lax.broadcasted_iota(jnp.int32, (rows, tile), 0)
        block = near[src_e, :, cols]
        masked = jnp.where(ids < live, block, jnp.zeros_like(block))
        acc[:, cols] += jnp.dot(left, masked, preferred_element_type=jnp.float32)

    def choose(src_e):
        which, live = 0, 0
        for k in range(n_hop):
            same = neighbours[k, e] == src_e
            which = jnp.where(same, k, which)
            live = jnp.where(same, counts[src_e], live)
        return which, live

    def apply_hop(src_e):
        which, live = choose(src_e)

        @pl.loop(0, width // tile)
        def _(n):
            add_product(n, hop_all[which].reshape(rows, rows), src_e, live)

    def apply_column(d, own):
        @pl.loop(0, 2 if d else 1)
        def _(i):
            shift = d * (1 - 2 * i)
            src_e = 2 * (z + shift) + (y if own else 1 - y)

            @pl.when((z + shift >= 0) & (z + shift < depth))
            def _():
                if not own:
                    for k in range(CHUNKS):
                        near_copy(y_send, src_e, k, y_dev).wait_recv()
                apply_hop(src_e)

    def finish_own():
        diag_copy(2 * x + 1 - c, 0, partner).wait_recv()
        diag_relay(False).wait_recv()
        off_copy(1 - c).wait_recv()
        amat[pl.ds(half, half), pl.ds(0, half)] = amat[pl.ds(0, half), pl.ds(half, half)].T

        @pl.loop(0, width // tile)
        def _(n):
            add_product(n, amat[...], e, counts[e])

    def out_copy(n):
        return pltpu.make_async_copy(acc.at[:, columns(n)], out.at[:, columns(n)], out_sem.at[n])

    def finish():
        at_end = (z == 0) | (z == depth - 1)
        src_e = 2 * (depth - 1 - z) + 1 - y
        which, live = choose(src_e)

        @pl.when(at_end)
        def _():
            for k in range(CHUNKS):
                near_copy(y_send, src_e, k, y_dev).wait_recv()

        @pl.loop(0, width // tile)
        def _(n):
            @pl.when(at_end)
            def _():
                add_product(n, hop_all[which].reshape(rows, rows), src_e, live)

            ids = lax.broadcasted_iota(jnp.int32, (rows, tile), 0)
            acc[:, columns(n)] = jnp.where(ids < counts[e], acc[:, columns(n)], 0.0)
            out_copy(n).start()

    do = functools.partial
    plan = {
        (1, 0): [diag_product],
        (1, 2): [diag_finish, do(hop_forward, 0)],
        (1, 4): [do(hop_forward, 1), do(send_piece, 1)],
        (1, 5): [do(hop_forward, 2)],
        (2, 0): [do(hop_forward, 3), diag_forward, do(send_piece, 2)],
        (2, 2): [hop_ready, do(apply_column, 0, False), do(send_piece, 3)],
        (2, 3): [do(off_piece, 0)],
        (2, 4): [do(apply_column, 1, True)],
        (3, 0): [do(off_piece, 1), do(apply_column, 1, False)],
        (3, 2): [do(off_piece, 2)],
        (3, 3): [do(apply_column, 2, True)],
        (3, 5): [do(off_piece, 3), off_sum, do(apply_column, 2, False), off_finish, finish_own],
    }

    nbr = 2 * z + 1 - y
    near_copy(y_send, nbr, CHUNKS, y_dev).wait_recv()
    to_right(nbr, CHUNKS, start)
    to_left(nbr, CHUNKS, start)

    for d in range(1, depth):
        for k in range(CHUNKS):
            @pl.when(z >= d)
            def _():
                near_copy(right_send, e - 2 * d, k, right).wait_recv()
                to_right(e - 2 * d, k, start)
                near_copy(y_send, e - 2 * d, k, y_dev).start()

            @pl.when(z + d < depth)
            def _():
                near_copy(left_send, e + 2 * d, k, left).wait_recv()
                to_left(e + 2 * d, k, start)
                near_copy(y_send, e + 2 * d, k, y_dev).start()

            for step in plan.get((d, k), ()):
                step()
        for base in (e, nbr):
            @pl.when(z >= d)
            def _():
                near_copy(right_send, base - 2 * d, CHUNKS, right).wait_recv()
                to_right(base - 2 * d, CHUNKS, start)

            @pl.when(z + d < depth)
            def _():
                near_copy(left_send, base + 2 * d, CHUNKS, left).wait_recv()
                to_left(base + 2 * d, CHUNKS, start)

    apply_column(3, True)
    finish()

    @pl.loop(0, width // tile)
    def _(n):
        out_copy(n).wait()

    pot_copy().wait_send()
    for arr in range(2):
        for which in range(2):
            pair_copy(which, arr, True).wait_send()
        for core in range(2):
            for k in range(PIECES):
                slab_copy(core, arr, k, True).wait_send()
    hop_pair(True).wait_send()
    for k in range(n_hop):
        hop_across(k, True).wait_send()
        hop_relay(k, True).wait_send()
    remote(acc_d.at[1 - c], got_d, red_send.at[0], red_recv.at[0], partner).wait_send()
    remote(acc_o.at[1 - c], got_o, red_send.at[1], red_recv.at[1], partner).wait_send()
    remote(low_o, got_x, red_send.at[2], red_recv.at[2], across).wait_send()
    diag_copy(g, 0, partner).wait_send()
    diag_copy(g, 1, across).wait_send()
    diag_relay(True).wait_send()
    off_copy(c).wait_send()
    near_copy(y_send, e, CHUNKS, y_dev).wait_send()

    @pl.loop(0, depth)
    def _(zz):
        src = 2 * zz + y
        for k in range(CHUNKS):
            near_copy(y_send, src, k, y_dev).wait_send()

        @pl.when(zz <= z)
        def _():
            for k in range(CHUNKS + 1):
                to_right(src, k, wait_send)
            to_right(2 * zz + 1 - y, CHUNKS, wait_send)

        @pl.when(zz >= z)
        def _():
            for k in range(CHUNKS + 1):
                to_left(src, k, wait_send)
            to_left(2 * zz + 1 - y, CHUNKS, wait_send)


def local_kernels(basis_values, basis_derivs, potential, hop_blocks, coeffs, counts, neighbours):
    n_elem = counts.shape[0]
    width, bands = coeffs.shape[1:]
    n_rows, n_points = basis_values.shape[1:]
    slab = potential.shape[1]
    n_hop = hop_blocks.shape[1]
    n_grp = width // n_rows
    half = 2 * n_rows
    bf16, f32 = jnp.bfloat16, jnp.float32
    anywhere = pl.BlockSpec(memory_space=pl.ANY)
    dma = pltpu.SemaphoreType.DMA
    vmem = pltpu.VMEM
    flops = 2 * half * half * 3 * 2 * slab
    smem = pl.BlockSpec(memory_space=pltpu.SMEM)
    out = pl.pallas_call(
        hamiltonian_kernel,
        out_shape=jax.ShapeDtypeStruct((width, bands), f32),
        in_specs=[anywhere] * 5 + [smem] * 2,
        out_specs=anywhere,
        scratch_shapes=[
            vmem((n_elem, width, bands), bf16), vmem((n_hop, n_grp, n_rows, width), bf16),
            vmem((width, width), bf16), vmem((width, bands), f32),
            vmem((n_grp, n_rows, slab), bf16), vmem((n_grp, n_rows, slab), bf16),
            vmem((2, n_rows, slab), bf16), vmem((2, n_rows, slab), bf16),
            vmem((2, 1, slab), f32),
            vmem((2, n_rows, half), f32), vmem((2, n_rows, half), f32),
            vmem((n_rows, half), f32), vmem((n_rows, half), f32), vmem((n_rows, half), f32),
            vmem((n_rows, half), bf16), vmem((n_rows, half), bf16),
            dma((7,)), dma((2, 2)), dma((2, 2)), dma((2, 2, PIECES)), dma((2, 2, PIECES)), dma((2,)),
            dma((3,)), dma((3,)), dma((3,)), dma((3,)), dma, dma,
            dma((1 + 2 * n_hop,)), dma((1 + 2 * n_hop,)),
            dma((n_elem, CHUNKS + 1)), dma((n_elem, CHUNKS + 1)),
            dma((n_elem, CHUNKS + 1)), dma((n_elem, CHUNKS + 1)), dma((bands // 256,)),
        ],
        compiler_params=pltpu.CompilerParams(
            collective_id=0, has_side_effects=True, vmem_limit_bytes=60 * 2 ** 20
        ),
        cost_estimate=pl.CostEstimate(
            flops=flops + 2 * n_elem * width * width * bands, bytes_accessed=2 ** 25, transcendentals=0
        ),
        name="hamiltonian",
    )(
        basis_values[0], basis_derivs[0], potential, hop_blocks[0], coeffs[0], counts, neighbours.T
    )
    return out[None]


def solution(mesh):
    placed = (
        P("elem", "grp", None),
        P("elem", "grp", None),
        P("elem", "grp"),
        P("elem", None, "grp", None),
        P("elem", None, "grp"),
        P(),
        P(),
    )
    fits = mesh.shape["elem"] == 8 and mesh.shape["grp"] == 4
    return jax.shard_map(
        local_kernels if fits else local,
        mesh=mesh, in_specs=placed, out_specs=P("elem", None, "grp"), check_vma=False,
    )
```

```python
import functools

import jax
import jax.numpy as jnp
from jax import lax
from jax.experimental import pallas as pl
from jax.experimental.pallas import tpu as pltpu
from jax.sharding import PartitionSpec as P


def local(basis_values, basis_derivs, potential, hop_blocks, coeffs, counts, neighbours):
    values_slab, derivs_slab = (
        lax.all_to_all(basis_values, "grp", split_axis=2, concat_axis=1, tiled=True),
        lax.all_to_all(basis_derivs, "grp", split_axis=2, concat_axis=1, tiled=True),
    )
    values_slab = values_slab[0]
    derivs_slab = derivs_slab[0]
    weighted = (potential[0][None, :] * values_slab.astype(jnp.float32)).astype(jnp.bfloat16)
    partial_value = 0.5 * jnp.einsum(
        "ip,jp->ij", derivs_slab, derivs_slab, preferred_element_type=jnp.float32
    )
    partial_value = partial_value + jnp.einsum(
        "ip,jp->ij", values_slab, weighted, preferred_element_type=jnp.float32
    )
    element = lax.axis_index("elem")
    width = coeffs.shape[1]
    row_ids = jnp.arange(width, dtype=jnp.int32)
    live_rows = row_ids < counts[element]
    own_coeffs = jnp.where(live_rows[:, None], coeffs[0], jnp.zeros_like(coeffs[0]))
    near_ids = neighbours[element]
    initial = jnp.zeros((near_ids.shape[0], width, coeffs.shape[2]), jnp.bfloat16)
    pieces = lax.all_gather(own_coeffs[None], "elem", axis=0, tiled=True)
    inside = (near_ids >= 0) & (near_ids < pieces.shape[0])
    clipped = jnp.clip(near_ids, 0, pieces.shape[0] - 1)
    picked = jnp.take(pieces, clipped, axis=0)
    near_coeffs = jnp.where(inside[:, None, None], picked, initial)
    assembled_low = lax.psum(partial_value, "grp").astype(jnp.bfloat16)
    applied = jnp.dot(assembled_low, own_coeffs, preferred_element_type=jnp.float32)
    applied = applied + jnp.einsum(
        "krm,kmb->rb",
        lax.all_gather(hop_blocks, "grp", axis=2, tiled=True)[0],
        near_coeffs,
        preferred_element_type=jnp.float32,
    )
    result = jnp.where(live_rows[:, None], applied, jnp.zeros_like(applied))
    return result[None]


NT = (((1,), (1,)), ((), ()))
PIECES = 4
CHUNKS = 6


def hamiltonian_kernel(
    values, derivs, pot, hop, coeffs, counts, neighbours, out,
    near, hop_all, amat, acc,
    vbuf, dbuf, vbuf2, dbuf2, potbuf, acc_d, acc_o, got_d, got_o, sum_o, low_o, got_x,
    load_sem, pair_send, pair_recv, slab_send, slab_recv, pot_sem, red_send, red_recv,
    diag_send, diag_recv, off_send, off_recv, hop_send, hop_recv,
    right_send, left_send, y_send, near_recv, out_sem,
):
    e = lax.axis_index("elem")
    g = lax.axis_index("grp")
    z, y = e // 2, e % 2
    x, c = g // 2, g % 2
    partner = {"grp": 2 * x + 1 - c}
    across = {"grp": 2 * (1 - x) + c}
    beyond = {"grp": 2 * (1 - x) + 1 - c}
    y_dev = {"elem": 2 * z + 1 - y}
    right = {"elem": e + 2}
    left = {"elem": e - 2}
    depth = 4
    rows, width = coeffs.shape
    part = rows * 9 // 64 // 16 * 16
    n_rows, slab = vbuf.shape[1], vbuf.shape[2]
    piece = slab // PIECES
    other_slab = 2 * (1 - x) + c

    def remote(src, dst, ss, rs, dev):
        return pltpu.make_async_remote_copy(
            src_ref=src, dst_ref=dst, send_sem=ss, recv_sem=rs,
            device_id=dev, device_id_type=pl.DeviceIdType.MESH,
        )

    barrier = pltpu.get_barrier_semaphore()
    for dev in (partner, across, beyond, y_dev):
        pl.semaphore_signal(barrier, inc=1, device_id=dev, device_id_type=pl.DeviceIdType.MESH)

    @pl.when(z < depth - 1)
    def _():
        pl.semaphore_signal(barrier, inc=1, device_id=right, device_id_type=pl.DeviceIdType.MESH)

    @pl.when(z > 0)
    def _():
        pl.semaphore_signal(barrier, inc=1, device_id=left, device_id_type=pl.DeviceIdType.MESH)

    pl.semaphore_wait(barrier, 4 + (z + depth - 2) // (depth - 1) + (2 * depth - 3 - z) // (depth - 1))

    def points(which, start, size):
        return pl.ds(pl.multiple_of(which * slab + start, 128), size)

    def slab_copy(core, arr, k, mine):
        src = (values, derivs)[arr].at[:, points(2 * (1 - x) + core, k * piece, piece)]
        row = g if mine else 2 * (1 - x) + core
        dst = (vbuf, dbuf)[arr].at[row, :, pl.ds(k * piece, piece)]
        return remote(
            src, dst, slab_send.at[core, arr, k],
            slab_recv.at[c if mine else core, arr, k], {"grp": 2 * (1 - x) + core},
        )

    def pair_copy(which, arr, mine):
        ref = (values, derivs)[arr]
        their = 1 - c if mine else c
        src = ref.at[:, points(2 * x + their if which == 0 else 2 * (1 - x) + their, 0, slab)]
        if which == 0:
            dst = (vbuf, dbuf)[arr].at[g if mine else 2 * x + 1 - c]
        else:
            dst = (vbuf2, dbuf2)[arr].at[c if mine else 1 - c]
        return remote(src, dst, pair_send.at[which, arr], pair_recv.at[which, arr], partner)

    def pot_copy():
        return remote(pot, potbuf.at[1], pot_sem.at[0], pot_sem.at[1], across)

    def send_piece(k):
        for arr in range(2):
            for core in range(2):
                slab_copy(core, arr, k, True).start()

    first = CHUNKS * part - 16

    def rows_of(k):
        if k < CHUNKS - 1:
            return pl.ds(k * part, part)
        if k == CHUNKS - 1:
            return pl.ds(k * part, first - k * part)
        return pl.ds(first, rows - first)

    def near_copy(sems, src_e, k, dev, own=False):
        src = coeffs.at[rows_of(k)] if own else near.at[src_e, rows_of(k)]
        return remote(src, near.at[src_e, rows_of(k)], sems.at[src_e, k], near_recv.at[src_e, k], dev)

    def to_right(src_e, k, act, own=False):
        @pl.when(z < depth - 1)
        def _():
            act(near_copy(right_send, src_e, k, right, own))

    def to_left(src_e, k, act, own=False):
        @pl.when(z > 0)
        def _():
            act(near_copy(left_send, src_e, k, left, own))

    def start(copy):
        copy.start()

    def wait_send(copy):
        copy.wait_send()

    n_hop = hop.shape[0]

    def hop_pair(mine):
        return remote(
            hop, hop_all.at[:, g if mine else 2 * x + 1 - c], hop_send.at[0], hop_recv.at[0], partner
        )

    def hop_across(k, mine):
        return remote(
            hop.at[k], hop_all.at[k, g if mine else 2 * (1 - x) + c],
            hop_send.at[1 + k], hop_recv.at[1 + k], across,
        )

    def hop_relay(k, mine):
        row = 2 * (1 - x) + (c if mine else 1 - c)
        ref = hop_all.at[k, row]
        return remote(ref, ref, hop_send.at[1 + n_hop + k], hop_recv.at[1 + n_hop + k], partner)

    pot_copy().start()
    for k in range(n_hop):
        hop_across(k, True).start()
    near_copy(y_send, e, CHUNKS, y_dev, True).start()
    for k in range(CHUNKS + 1):
        to_right(e, k, start, True)
        to_left(e, k, start, True)
        if k < CHUNKS:
            near_copy(y_send, e, k, y_dev, True).start()

    loads = []

    def load(src, dst):
        copy = pltpu.make_async_copy(src, dst, load_sem.at[len(loads)])
        copy.start()
        loads.append(copy)

    for arr in range(2):
        for which in range(2):
            pair_copy(which, arr, True).start()
    for arr in range(2):
        ref = (values, derivs)[arr]
        load(ref.at[:, points(g, 0, slab)], (vbuf, dbuf)[arr].at[g])
        load(ref.at[:, points(other_slab, 0, slab)], (vbuf2, dbuf2)[arr].at[c])
    load(pot, potbuf.at[0])
    load(coeffs, near.at[e])
    load(hop, hop_all.at[:, g])
    hop_pair(True).start()
    send_piece(0)
    send_piece(1)
    acc[...] = jnp.zeros_like(acc)

    def product(v_low, d_low, v_high, d_high, weight):
        weighted = (weight * v_high.astype(jnp.float32)).astype(jnp.bfloat16)
        out = 0.5 * lax.dot_general(d_low, d_high, NT, preferred_element_type=jnp.float32)
        return out + lax.dot_general(v_low, weighted, NT, preferred_element_type=jnp.float32)

    half = 2 * n_rows

    def two(ref, first, cols):
        return ref[pl.ds(first, 2), :, cols].reshape(half, piece)

    def diag_product():
        for copy in loads[:5]:
            copy.wait()
        for arr in range(2):
            for which in range(2):
                pair_copy(which, arr, False).wait_recv()
        pot_copy().wait_recv()
        acc_d[...] = jnp.zeros_like(acc_d)

        @pl.loop(0, PIECES)
        def _(k):
            cols = pl.ds(pl.multiple_of(k * piece, 128), piece)
            for vb, db, first, which in ((vbuf, dbuf, 2 * x, 0), (vbuf2, dbuf2, 0, 1)):
                v = two(vb, first, cols)
                d = two(db, first, cols)
                acc_d[...] += product(v, d, v, d, potbuf[which, :, cols]).reshape(acc_d.shape)

        remote(acc_d.at[1 - c], got_d, red_send.at[0], red_recv.at[0], partner).start()

    def diag_block(row):
        cols = pl.ds(pl.multiple_of(row // 2 * half, 128), half)
        return amat.at[pl.ds(pl.multiple_of(row * n_rows, 16), n_rows), cols]

    def diag_copy(row, which, dev):
        ref = diag_block(row)
        return remote(ref, ref, diag_send.at[which], diag_recv.at[which], dev)

    def diag_finish():
        remote(acc_d.at[1 - c], got_d, red_send.at[0], red_recv.at[0], partner).wait_recv()
        diag_block(g)[...] = (acc_d[c] + got_d[...]).astype(jnp.bfloat16)
        diag_copy(g, 0, partner).start()
        diag_copy(g, 1, across).start()

    def diag_relay(mine):
        return diag_copy(2 * (1 - x) + (c if mine else 1 - c), 2, partner)

    def diag_forward():
        diag_copy(2 * (1 - x) + c, 1, across).wait_recv()
        diag_relay(True).start()

    def off_piece(k):
        for arr in range(2):
            for core in range(2):
                slab_copy(core, arr, k, False).wait_recv()
        cols = pl.ds(k * piece, piece)
        term = product(
            two(vbuf, 0, cols), two(dbuf, 0, cols), two(vbuf, 2, cols), two(dbuf, 2, cols),
            potbuf[0, :, cols],
        ).reshape(acc_o.shape)
        if k == 0:
            acc_o[...] = term
        else:
            acc_o[...] += term
        if k == PIECES - 1:
            for h in range(2):
                core_copy(h).start()

    halves = [pl.ds(h * (n_rows // 2), n_rows // 2) for h in range(2)]

    def core_copy(h):
        return remote(
            acc_o.at[1 - c, halves[h]], got_o.at[halves[h]], red_send.at[1 + h], red_recv.at[1 + h], partner
        )

    def sum_copy(h):
        return remote(
            low_o.at[halves[h]], got_x.at[halves[h]], red_send.at[3 + h], red_recv.at[3 + h], across
        )

    def off_copy(row, h):
        here = pl.ds(pl.multiple_of(row * n_rows + h * (n_rows // 2), 16), n_rows // 2)
        ref = amat.at[here, pl.ds(half, half)]
        return remote(ref, ref, off_send.at[h], off_recv.at[h], partner)

    def off_sum():
        for h in range(2):
            core_copy(h).wait_recv()
            sum_o[halves[h]] = acc_o[c, halves[h]] + got_o[halves[h]]
            low_o[halves[h]] = sum_o[halves[h]].astype(jnp.bfloat16)
            sum_copy(h).start()

    def off_finish():
        for h in range(2):
            sum_copy(h).wait_recv()
            here = pl.ds(pl.multiple_of(c * n_rows + h * (n_rows // 2), 16), n_rows // 2)
            total = sum_o[halves[h]] + got_x[halves[h]].astype(jnp.float32)
            amat[here, pl.ds(half, half)] = total.astype(jnp.bfloat16)
            off_copy(c, h).start()

    def hop_forward(k):
        hop_across(k, False).wait_recv()
        hop_relay(k, True).start()

    def hop_ready():
        hop_pair(False).wait_recv()
        for k in range(n_hop):
            hop_relay(k, False).wait_recv()
        loads[5].wait()
        loads[6].wait()

    tile = 256

    def columns(n):
        return pl.ds(pl.multiple_of(n * tile, tile), tile)

    def add_product(n, left, src_e, live):
        cols = columns(n)
        ids = lax.broadcasted_iota(jnp.int32, (rows, tile), 0)
        block = near[src_e, :, cols]
        masked = jnp.where(ids < live, block, jnp.zeros_like(block))
        acc[:, cols] += jnp.dot(left, masked, preferred_element_type=jnp.float32)

    def choose(src_e):
        which, live = 0, 0
        for k in range(n_hop):
            same = neighbours[k, e] == src_e
            which = jnp.where(same, k, which)
            live = jnp.where(same, counts[src_e], live)
        return which, live

    def apply_hop(src_e):
        which, live = choose(src_e)

        @pl.loop(0, width // tile)
        def _(n):
            add_product(n, hop_all[which].reshape(rows, rows), src_e, live)

    def apply_column(d, own):
        @pl.loop(0, 2 if d else 1)
        def _(i):
            shift = d * (1 - 2 * i)
            src_e = 2 * (z + shift) + (y if own else 1 - y)

            @pl.when((z + shift >= 0) & (z + shift < depth))
            def _():
                if not own:
                    for k in range(CHUNKS):
                        near_copy(y_send, src_e, k, y_dev).wait_recv()
                apply_hop(src_e)

    low, high = pl.ds(0, half), pl.ds(half, half)

    def add_blocks(row_blocks):
        @pl.loop(0, width // tile)
        def _(n):
            cols = columns(n)
            for here, there in row_blocks:
                ids = lax.broadcasted_iota(jnp.int32, (half, tile), 0) + there.start
                block = near[e, there, cols]
                masked = jnp.where(ids < counts[e], block, jnp.zeros_like(block))
                acc[here, cols] += jnp.dot(amat[here, there], masked, preferred_element_type=jnp.float32)

    def apply_diag():
        diag_copy(2 * x + 1 - c, 0, partner).wait_recv()
        diag_relay(False).wait_recv()
        add_blocks([(low, low), (high, high)])

    def finish_own():
        for h in range(2):
            off_copy(1 - c, h).wait_recv()
        amat[high, low] = amat[low, high].T
        add_blocks([(low, high), (high, low)])

    def out_copy(n):
        return pltpu.make_async_copy(acc.at[:, columns(n)], out.at[:, columns(n)], out_sem.at[n])

    def finish():
        at_end = (z == 0) | (z == depth - 1)
        src_e = 2 * (depth - 1 - z) + 1 - y
        which, live = choose(src_e)

        @pl.when(at_end)
        def _():
            for k in range(CHUNKS):
                near_copy(y_send, src_e, k, y_dev).wait_recv()

        @pl.loop(0, width // tile)
        def _(n):
            @pl.when(at_end)
            def _():
                add_product(n, hop_all[which].reshape(rows, rows), src_e, live)

            ids = lax.broadcasted_iota(jnp.int32, (rows, tile), 0)
            acc[:, columns(n)] = jnp.where(ids < counts[e], acc[:, columns(n)], 0.0)
            out_copy(n).start()

    do = functools.partial
    plan = {
        (1, 0): [diag_product],
        (1, 2): [diag_finish, do(hop_forward, 0), do(send_piece, 2)],
        (1, 4): [do(hop_forward, 1)],
        (1, 5): [do(hop_forward, 2), do(send_piece, 3)],
        (2, 0): [do(hop_forward, 3)],
        (2, 2): [hop_ready, do(apply_column, 0, False)],
        (2, 3): [do(off_piece, 0)],
        (2, 4): [do(apply_column, 1, True)],
        (3, 0): [do(off_piece, 1), do(apply_column, 1, False)],
        (3, 2): [do(off_piece, 2)],
        (3, 3): [do(apply_column, 2, True)],
        (3, 5): [
            do(off_piece, 3), off_sum, diag_forward, do(apply_column, 2, False), apply_diag, off_finish,
            finish_own,
        ],
    }

    nbr = 2 * z + 1 - y
    near_copy(y_send, nbr, CHUNKS, y_dev).wait_recv()
    to_right(nbr, CHUNKS, start)
    to_left(nbr, CHUNKS, start)

    for d in range(1, depth):
        for k in range(CHUNKS):
            @pl.when(z >= d)
            def _():
                near_copy(right_send, e - 2 * d, k, right).wait_recv()
                to_right(e - 2 * d, k, start)
                near_copy(y_send, e - 2 * d, k, y_dev).start()

            @pl.when(z + d < depth)
            def _():
                near_copy(left_send, e + 2 * d, k, left).wait_recv()
                to_left(e + 2 * d, k, start)
                near_copy(y_send, e + 2 * d, k, y_dev).start()

            for step in plan.get((d, k), ()):
                step()
        for base in (e, nbr):
            @pl.when(z >= d)
            def _():
                near_copy(right_send, base - 2 * d, CHUNKS, right).wait_recv()
                to_right(base - 2 * d, CHUNKS, start)

            @pl.when(z + d < depth)
            def _():
                near_copy(left_send, base + 2 * d, CHUNKS, left).wait_recv()
                to_left(base + 2 * d, CHUNKS, start)

    apply_column(3, True)
    finish()

    @pl.loop(0, width // tile)
    def _(n):
        out_copy(n).wait()

    pot_copy().wait_send()
    for arr in range(2):
        for which in range(2):
            pair_copy(which, arr, True).wait_send()
        for core in range(2):
            for k in range(PIECES):
                slab_copy(core, arr, k, True).wait_send()
    hop_pair(True).wait_send()
    for k in range(n_hop):
        hop_across(k, True).wait_send()
        hop_relay(k, True).wait_send()
    remote(acc_d.at[1 - c], got_d, red_send.at[0], red_recv.at[0], partner).wait_send()
    for h in range(2):
        core_copy(h).wait_send()
        sum_copy(h).wait_send()
        off_copy(c, h).wait_send()
    diag_copy(g, 0, partner).wait_send()
    diag_copy(g, 1, across).wait_send()
    diag_relay(True).wait_send()
    near_copy(y_send, e, CHUNKS, y_dev).wait_send()

    @pl.loop(0, depth)
    def _(zz):
        src = 2 * zz + y
        for k in range(CHUNKS):
            near_copy(y_send, src, k, y_dev).wait_send()

        @pl.when(zz <= z)
        def _():
            for k in range(CHUNKS + 1):
                to_right(src, k, wait_send)
            to_right(2 * zz + 1 - y, CHUNKS, wait_send)

        @pl.when(zz >= z)
        def _():
            for k in range(CHUNKS + 1):
                to_left(src, k, wait_send)
            to_left(2 * zz + 1 - y, CHUNKS, wait_send)


def local_kernels(basis_values, basis_derivs, potential, hop_blocks, coeffs, counts, neighbours):
    n_elem = counts.shape[0]
    width, bands = coeffs.shape[1:]
    n_rows, n_points = basis_values.shape[1:]
    slab = potential.shape[1]
    n_hop = hop_blocks.shape[1]
    n_grp = width // n_rows
    half = 2 * n_rows
    bf16, f32 = jnp.bfloat16, jnp.float32
    anywhere = pl.BlockSpec(memory_space=pl.ANY)
    dma = pltpu.SemaphoreType.DMA
    vmem = pltpu.VMEM
    flops = 2 * half * half * 3 * 2 * slab
    smem = pl.BlockSpec(memory_space=pltpu.SMEM)
    out = pl.pallas_call(
        hamiltonian_kernel,
        out_shape=jax.ShapeDtypeStruct((width, bands), f32),
        in_specs=[anywhere] * 5 + [smem] * 2,
        out_specs=anywhere,
        scratch_shapes=[
            vmem((n_elem, width, bands), bf16), vmem((n_hop, n_grp, n_rows, width), bf16),
            vmem((width, width), bf16), vmem((width, bands), f32),
            vmem((n_grp, n_rows, slab), bf16), vmem((n_grp, n_rows, slab), bf16),
            vmem((2, n_rows, slab), bf16), vmem((2, n_rows, slab), bf16),
            vmem((2, 1, slab), f32),
            vmem((2, n_rows, half), f32), vmem((2, n_rows, half), f32),
            vmem((n_rows, half), f32), vmem((n_rows, half), f32), vmem((n_rows, half), f32),
            vmem((n_rows, half), bf16), vmem((n_rows, half), bf16),
            dma((7,)), dma((2, 2)), dma((2, 2)), dma((2, 2, PIECES)), dma((2, 2, PIECES)), dma((2,)),
            dma((5,)), dma((5,)), dma((3,)), dma((3,)), dma((2,)), dma((2,)),
            dma((1 + 2 * n_hop,)), dma((1 + 2 * n_hop,)),
            dma((n_elem, CHUNKS + 1)), dma((n_elem, CHUNKS + 1)),
            dma((n_elem, CHUNKS + 1)), dma((n_elem, CHUNKS + 1)), dma((bands // 256,)),
        ],
        compiler_params=pltpu.CompilerParams(
            collective_id=0, has_side_effects=True, vmem_limit_bytes=60 * 2 ** 20
        ),
        cost_estimate=pl.CostEstimate(
            flops=flops + 2 * n_elem * width * width * bands, bytes_accessed=2 ** 25, transcendentals=0
        ),
        name="hamiltonian",
    )(
        basis_values[0], basis_derivs[0], potential, hop_blocks[0], coeffs[0], counts, neighbours.T
    )
    return out[None]


def solution(mesh):
    placed = (
        P("elem", "grp", None),
        P("elem", "grp", None),
        P("elem", "grp"),
        P("elem", None, "grp", None),
        P("elem", None, "grp"),
        P(),
        P(),
    )
    fits = mesh.shape["elem"] == 8 and mesh.shape["grp"] == 4
    return jax.shard_map(
        local_kernels if fits else local,
        mesh=mesh, in_specs=placed, out_specs=P("elem", None, "grp"), check_vma=False,
    )
```

```python
import functools

import jax
import jax.numpy as jnp
from jax import lax
from jax.experimental import pallas as pl
from jax.experimental.pallas import tpu as pltpu
from jax.sharding import PartitionSpec as P


def local(basis_values, basis_derivs, potential, hop_blocks, coeffs, counts, neighbours):
    values_slab, derivs_slab = (
        lax.all_to_all(basis_values, "grp", split_axis=2, concat_axis=1, tiled=True),
        lax.all_to_all(basis_derivs, "grp", split_axis=2, concat_axis=1, tiled=True),
    )
    values_slab = values_slab[0]
    derivs_slab = derivs_slab[0]
    weighted = (potential[0][None, :] * values_slab.astype(jnp.float32)).astype(jnp.bfloat16)
    partial_value = 0.5 * jnp.einsum(
        "ip,jp->ij", derivs_slab, derivs_slab, preferred_element_type=jnp.float32
    )
    partial_value = partial_value + jnp.einsum(
        "ip,jp->ij", values_slab, weighted, preferred_element_type=jnp.float32
    )
    element = lax.axis_index("elem")
    width = coeffs.shape[1]
    row_ids = jnp.arange(width, dtype=jnp.int32)
    live_rows = row_ids < counts[element]
    own_coeffs = jnp.where(live_rows[:, None], coeffs[0], jnp.zeros_like(coeffs[0]))
    near_ids = neighbours[element]
    initial = jnp.zeros((near_ids.shape[0], width, coeffs.shape[2]), jnp.bfloat16)
    pieces = lax.all_gather(own_coeffs[None], "elem", axis=0, tiled=True)
    inside = (near_ids >= 0) & (near_ids < pieces.shape[0])
    clipped = jnp.clip(near_ids, 0, pieces.shape[0] - 1)
    picked = jnp.take(pieces, clipped, axis=0)
    near_coeffs = jnp.where(inside[:, None, None], picked, initial)
    assembled_low = lax.psum(partial_value, "grp").astype(jnp.bfloat16)
    applied = jnp.dot(assembled_low, own_coeffs, preferred_element_type=jnp.float32)
    applied = applied + jnp.einsum(
        "krm,kmb->rb",
        lax.all_gather(hop_blocks, "grp", axis=2, tiled=True)[0],
        near_coeffs,
        preferred_element_type=jnp.float32,
    )
    result = jnp.where(live_rows[:, None], applied, jnp.zeros_like(applied))
    return result[None]


NT = (((1,), (1,)), ((), ()))
PIECES = 4
CHUNKS = 6


def hamiltonian_kernel(
    values, derivs, pot, hop, coeffs, counts, neighbours, out,
    near, hop_all, amat, acc,
    vbuf, dbuf, vbuf2, dbuf2, potbuf, acc_d, acc_o, got_d, got_o, sum_o, low_o, got_x,
    load_sem, pair_send, pair_recv, slab_send, slab_recv, pot_sem, red_send, red_recv,
    diag_send, diag_recv, off_send, off_recv, hop_send, hop_recv,
    right_send, left_send, y_send, near_recv, out_sem,
):
    e = lax.axis_index("elem")
    g = lax.axis_index("grp")
    z, y = e // 2, e % 2
    x, c = g // 2, g % 2
    partner = {"grp": 2 * x + 1 - c}
    across = {"grp": 2 * (1 - x) + c}
    beyond = {"grp": 2 * (1 - x) + 1 - c}
    y_dev = {"elem": 2 * z + 1 - y}
    right = {"elem": e + 2}
    left = {"elem": e - 2}
    depth = 4
    rows, width = coeffs.shape
    part = rows * 9 // 64 // 16 * 16
    n_rows, slab = vbuf.shape[1], vbuf.shape[2]
    piece = slab // PIECES
    other_slab = 2 * (1 - x) + c

    def remote(src, dst, ss, rs, dev):
        return pltpu.make_async_remote_copy(
            src_ref=src, dst_ref=dst, send_sem=ss, recv_sem=rs,
            device_id=dev, device_id_type=pl.DeviceIdType.MESH,
        )

    barrier = pltpu.get_barrier_semaphore()
    for dev in (partner, across, beyond, y_dev):
        pl.semaphore_signal(barrier, inc=1, device_id=dev, device_id_type=pl.DeviceIdType.MESH)

    @pl.when(z < depth - 1)
    def _():
        pl.semaphore_signal(barrier, inc=1, device_id=right, device_id_type=pl.DeviceIdType.MESH)

    @pl.when(z > 0)
    def _():
        pl.semaphore_signal(barrier, inc=1, device_id=left, device_id_type=pl.DeviceIdType.MESH)

    pl.semaphore_wait(barrier, 4 + (z + depth - 2) // (depth - 1) + (2 * depth - 3 - z) // (depth - 1))

    def points(which, start, size):
        return pl.ds(pl.multiple_of(which * slab + start, 128), size)

    def slab_copy(core, arr, k, mine):
        src = (values, derivs)[arr].at[:, points(2 * (1 - x) + core, k * piece, piece)]
        row = g if mine else 2 * (1 - x) + core
        dst = (vbuf, dbuf)[arr].at[row, :, pl.ds(k * piece, piece)]
        return remote(
            src, dst, slab_send.at[core, arr, k],
            slab_recv.at[c if mine else core, arr, k], {"grp": 2 * (1 - x) + core},
        )

    def pair_copy(which, arr, mine):
        ref = (values, derivs)[arr]
        their = 1 - c if mine else c
        src = ref.at[:, points(2 * x + their if which == 0 else 2 * (1 - x) + their, 0, slab)]
        if which == 0:
            dst = (vbuf, dbuf)[arr].at[g if mine else 2 * x + 1 - c]
        else:
            dst = (vbuf2, dbuf2)[arr].at[c if mine else 1 - c]
        return remote(src, dst, pair_send.at[which, arr], pair_recv.at[which, arr], partner)

    def pot_copy():
        return remote(pot, potbuf.at[1], pot_sem.at[0], pot_sem.at[1], across)

    def send_piece(k):
        for arr in range(2):
            for core in range(2):
                slab_copy(core, arr, k, True).start()

    first = CHUNKS * part - 16

    def rows_of(k):
        if k < CHUNKS - 1:
            return pl.ds(k * part, part)
        if k == CHUNKS - 1:
            return pl.ds(k * part, first - k * part)
        return pl.ds(first, rows - first)

    def near_copy(sems, src_e, k, dev, own=False):
        src = coeffs.at[rows_of(k)] if own else near.at[src_e, rows_of(k)]
        return remote(src, near.at[src_e, rows_of(k)], sems.at[src_e, k], near_recv.at[src_e, k], dev)

    def to_right(src_e, k, act, own=False):
        @pl.when(z < depth - 1)
        def _():
            act(near_copy(right_send, src_e, k, right, own))

    def to_left(src_e, k, act, own=False):
        @pl.when(z > 0)
        def _():
            act(near_copy(left_send, src_e, k, left, own))

    def start(copy):
        copy.start()

    def wait_send(copy):
        copy.wait_send()

    n_hop = hop.shape[0]

    def hop_pair(mine):
        return remote(
            hop, hop_all.at[:, g if mine else 2 * x + 1 - c], hop_send.at[0], hop_recv.at[0], partner
        )

    def hop_across(k, mine):
        return remote(
            hop.at[k], hop_all.at[k, g if mine else 2 * (1 - x) + c],
            hop_send.at[1 + k], hop_recv.at[1 + k], across,
        )

    def hop_relay(k, mine):
        row = 2 * (1 - x) + (c if mine else 1 - c)
        ref = hop_all.at[k, row]
        return remote(ref, ref, hop_send.at[1 + n_hop + k], hop_recv.at[1 + n_hop + k], partner)

    pot_copy().start()
    for k in range(n_hop):
        hop_across(k, True).start()
    near_copy(y_send, e, CHUNKS, y_dev, True).start()
    for k in range(CHUNKS + 1):
        to_right(e, k, start, True)
        to_left(e, k, start, True)
        if k < CHUNKS:
            near_copy(y_send, e, k, y_dev, True).start()

    loads = []

    def load(src, dst):
        copy = pltpu.make_async_copy(src, dst, load_sem.at[len(loads)])
        copy.start()
        loads.append(copy)

    for arr in range(2):
        for which in range(2):
            pair_copy(which, arr, True).start()
    for arr in range(2):
        ref = (values, derivs)[arr]
        load(ref.at[:, points(g, 0, slab)], (vbuf, dbuf)[arr].at[g])
        load(ref.at[:, points(other_slab, 0, slab)], (vbuf2, dbuf2)[arr].at[c])
    load(pot, potbuf.at[0])
    load(coeffs, near.at[e])
    load(hop, hop_all.at[:, g])
    hop_pair(True).start()
    send_piece(0)
    acc[...] = jnp.zeros_like(acc)

    def product(v_low, d_low, v_high, d_high, weight):
        weighted = (weight * v_high.astype(jnp.float32)).astype(jnp.bfloat16)
        out = 0.5 * lax.dot_general(d_low, d_high, NT, preferred_element_type=jnp.float32)
        return out + lax.dot_general(v_low, weighted, NT, preferred_element_type=jnp.float32)

    half = 2 * n_rows

    def two(ref, first, cols):
        return ref[pl.ds(first, 2), :, cols].reshape(half, piece)

    def diag_product():
        for copy in loads[:5]:
            copy.wait()
        for arr in range(2):
            for which in range(2):
                pair_copy(which, arr, False).wait_recv()
        pot_copy().wait_recv()
        acc_d[...] = jnp.zeros_like(acc_d)

        @pl.loop(0, PIECES)
        def _(k):
            cols = pl.ds(pl.multiple_of(k * piece, 128), piece)
            for vb, db, first, which in ((vbuf, dbuf, 2 * x, 0), (vbuf2, dbuf2, 0, 1)):
                v = two(vb, first, cols)
                d = two(db, first, cols)
                acc_d[...] += product(v, d, v, d, potbuf[which, :, cols]).reshape(acc_d.shape)

        remote(acc_d.at[1 - c], got_d, red_send.at[0], red_recv.at[0], partner).start()

    def diag_block(row):
        cols = pl.ds(pl.multiple_of(row // 2 * half, 128), half)
        return amat.at[pl.ds(pl.multiple_of(row * n_rows, 16), n_rows), cols]

    def diag_copy(row, which, dev):
        ref = diag_block(row)
        return remote(ref, ref, diag_send.at[which], diag_recv.at[which], dev)

    def diag_finish():
        remote(acc_d.at[1 - c], got_d, red_send.at[0], red_recv.at[0], partner).wait_recv()
        diag_block(g)[...] = (acc_d[c] + got_d[...]).astype(jnp.bfloat16)
        diag_copy(g, 0, partner).start()
        diag_copy(g, 1, across).start()

    def diag_relay(mine):
        return diag_copy(2 * (1 - x) + (c if mine else 1 - c), 2, partner)

    def diag_forward():
        diag_copy(2 * (1 - x) + c, 1, across).wait_recv()
        diag_relay(True).start()

    def off_copy(row):
        ref = amat.at[pl.ds(pl.multiple_of(row * n_rows, 16), n_rows), pl.ds(half, half)]
        return remote(ref, ref, off_send, off_recv, partner)

    def off_piece(k):
        for arr in range(2):
            for core in range(2):
                slab_copy(core, arr, k, False).wait_recv()
        cols = pl.ds(k * piece, piece)
        term = product(
            two(vbuf, 0, cols), two(dbuf, 0, cols), two(vbuf, 2, cols), two(dbuf, 2, cols),
            potbuf[0, :, cols],
        ).reshape(acc_o.shape)
        if k == 0:
            acc_o[...] = term
        else:
            acc_o[...] += term
        if k == PIECES - 1:
            remote(acc_o.at[1 - c], got_o, red_send.at[1], red_recv.at[1], partner).start()

    def off_sum():
        remote(acc_o.at[1 - c], got_o, red_send.at[1], red_recv.at[1], partner).wait_recv()
        sum_o[...] = acc_o[c] + got_o[...]
        low_o[...] = sum_o[...].astype(jnp.bfloat16)
        remote(low_o, got_x, red_send.at[2], red_recv.at[2], across).start()

    def off_finish():
        remote(low_o, got_x, red_send.at[2], red_recv.at[2], across).wait_recv()
        block = pl.ds(pl.multiple_of(c * n_rows, 16), n_rows)
        total = sum_o[...] + got_x[...].astype(jnp.float32)
        amat[block, pl.ds(half, half)] = total.astype(jnp.bfloat16)
        off_copy(c).start()

    def hop_forward(k):
        hop_across(k, False).wait_recv()
        hop_relay(k, True).start()

    def hop_ready():
        hop_pair(False).wait_recv()
        for k in range(n_hop):
            hop_relay(k, False).wait_recv()
        loads[5].wait()
        loads[6].wait()

    tile = 256

    def columns(n):
        return pl.ds(pl.multiple_of(n * tile, tile), tile)

    def add_product(n, left, src_e, live, lo=0, hi=rows):
        cols = columns(n)
        ids = lax.broadcasted_iota(jnp.int32, (hi - lo, tile), 0) + lo
        block = near[src_e, pl.ds(lo, hi - lo), cols]
        masked = jnp.where(ids < live, block, jnp.zeros_like(block))
        acc[:, cols] += jnp.dot(left[:, lo:hi], masked, preferred_element_type=jnp.float32)

    def choose(src_e):
        which, live = 0, 0
        for k in range(n_hop):
            same = neighbours[k, e] == src_e
            which = jnp.where(same, k, which)
            live = jnp.where(same, counts[src_e], live)
        return which, live

    def apply_hop(src_e):
        which, live = choose(src_e)

        @pl.loop(0, width // tile)
        def _(n):
            add_product(n, hop_all[which].reshape(rows, rows), src_e, live)

    def apply_column(d, own):
        @pl.loop(0, 2 if d else 1)
        def _(i):
            shift = d * (1 - 2 * i)
            src_e = 2 * (z + shift) + (y if own else 1 - y)

            @pl.when((z + shift >= 0) & (z + shift < depth))
            def _():
                if not own:
                    for k in range(CHUNKS):
                        near_copy(y_send, src_e, k, y_dev).wait_recv()
                apply_hop(src_e)

    def finish_own():
        diag_copy(2 * x + 1 - c, 0, partner).wait_recv()
        diag_relay(False).wait_recv()
        off_copy(1 - c).wait_recv()
        amat[pl.ds(half, half), pl.ds(0, half)] = amat[pl.ds(0, half), pl.ds(half, half)].T

        @pl.loop(0, width // tile)
        def _(n):
            add_product(n, amat[...], e, counts[e])

    def out_copy(n):
        return pltpu.make_async_copy(acc.at[:, columns(n)], out.at[:, columns(n)], out_sem.at[n])

    at_end = (z == 0) | (z == depth - 1)
    far = [2 * (depth - 1 - z) + y, 2 * (depth - 1 - z) + 1 - y]
    split = first // tile * tile

    def add_far(n, src_e, lo, hi):
        which, live = choose(src_e)
        add_product(n, hop_all[which].reshape(rows, rows), src_e, live, lo, hi)

    def far_first():
        @pl.when(at_end)
        def _():
            @pl.loop(0, width // tile)
            def _(n):
                add_far(n, far[0], 0, split)

            for k in range(CHUNKS):
                near_copy(y_send, far[1], k, y_dev).wait_recv()

            @pl.loop(0, width // tile)
            def _(n):
                add_far(n, far[1], 0, split)

    def finish():
        @pl.loop(0, width // tile)
        def _(n):
            @pl.when(at_end)
            def _():
                for src_e in far:
                    add_far(n, src_e, split, rows)

            ids = lax.broadcasted_iota(jnp.int32, (rows, tile), 0)
            acc[:, columns(n)] = jnp.where(ids < counts[e], acc[:, columns(n)], 0.0)
            out_copy(n).start()

    do = functools.partial
    plan = {
        (1, 0): [diag_product],
        (1, 2): [diag_finish, do(hop_forward, 0)],
        (1, 4): [do(hop_forward, 1), do(send_piece, 1)],
        (1, 5): [do(hop_forward, 2)],
        (2, 0): [do(hop_forward, 3), diag_forward, do(send_piece, 2)],
        (2, 2): [hop_ready, do(apply_column, 0, False), do(send_piece, 3)],
        (2, 3): [do(off_piece, 0)],
        (2, 4): [do(apply_column, 1, True)],
        (3, 0): [do(off_piece, 1), do(apply_column, 1, False)],
        (3, 2): [do(off_piece, 2)],
        (3, 3): [do(apply_column, 2, True)],
        (3, 5): [do(off_piece, 3), off_sum, do(apply_column, 2, False), off_finish, finish_own, far_first],
    }

    nbr = 2 * z + 1 - y
    near_copy(y_send, nbr, CHUNKS, y_dev).wait_recv()
    to_right(nbr, CHUNKS, start)
    to_left(nbr, CHUNKS, start)

    for d in range(1, depth):
        for k in range(CHUNKS):
            @pl.when(z >= d)
            def _():
                near_copy(right_send, e - 2 * d, k, right).wait_recv()
                to_right(e - 2 * d, k, start)
                near_copy(y_send, e - 2 * d, k, y_dev).start()

            @pl.when(z + d < depth)
            def _():
                near_copy(left_send, e + 2 * d, k, left).wait_recv()
                to_left(e + 2 * d, k, start)
                near_copy(y_send, e + 2 * d, k, y_dev).start()

            for step in plan.get((d, k), ()):
                step()
        for base in (e, nbr):
            @pl.when(z >= d)
            def _():
                near_copy(right_send, base - 2 * d, CHUNKS, right).wait_recv()
                to_right(base - 2 * d, CHUNKS, start)

            @pl.when(z + d < depth)
            def _():
                near_copy(left_send, base + 2 * d, CHUNKS, left).wait_recv()
                to_left(base + 2 * d, CHUNKS, start)

    finish()

    @pl.loop(0, width // tile)
    def _(n):
        out_copy(n).wait()

    pot_copy().wait_send()
    for arr in range(2):
        for which in range(2):
            pair_copy(which, arr, True).wait_send()
        for core in range(2):
            for k in range(PIECES):
                slab_copy(core, arr, k, True).wait_send()
    hop_pair(True).wait_send()
    for k in range(n_hop):
        hop_across(k, True).wait_send()
        hop_relay(k, True).wait_send()
    remote(acc_d.at[1 - c], got_d, red_send.at[0], red_recv.at[0], partner).wait_send()
    remote(acc_o.at[1 - c], got_o, red_send.at[1], red_recv.at[1], partner).wait_send()
    remote(low_o, got_x, red_send.at[2], red_recv.at[2], across).wait_send()
    diag_copy(g, 0, partner).wait_send()
    diag_copy(g, 1, across).wait_send()
    diag_relay(True).wait_send()
    off_copy(c).wait_send()
    near_copy(y_send, e, CHUNKS, y_dev).wait_send()

    @pl.loop(0, depth)
    def _(zz):
        src = 2 * zz + y
        for k in range(CHUNKS):
            near_copy(y_send, src, k, y_dev).wait_send()

        @pl.when(zz <= z)
        def _():
            for k in range(CHUNKS + 1):
                to_right(src, k, wait_send)
            to_right(2 * zz + 1 - y, CHUNKS, wait_send)

        @pl.when(zz >= z)
        def _():
            for k in range(CHUNKS + 1):
                to_left(src, k, wait_send)
            to_left(2 * zz + 1 - y, CHUNKS, wait_send)


def local_kernels(basis_values, basis_derivs, potential, hop_blocks, coeffs, counts, neighbours):
    n_elem = counts.shape[0]
    width, bands = coeffs.shape[1:]
    n_rows, n_points = basis_values.shape[1:]
    slab = potential.shape[1]
    n_hop = hop_blocks.shape[1]
    n_grp = width // n_rows
    half = 2 * n_rows
    bf16, f32 = jnp.bfloat16, jnp.float32
    anywhere = pl.BlockSpec(memory_space=pl.ANY)
    dma = pltpu.SemaphoreType.DMA
    vmem = pltpu.VMEM
    flops = 2 * half * half * 3 * 2 * slab
    smem = pl.BlockSpec(memory_space=pltpu.SMEM)
    out = pl.pallas_call(
        hamiltonian_kernel,
        out_shape=jax.ShapeDtypeStruct((width, bands), f32),
        in_specs=[anywhere] * 5 + [smem] * 2,
        out_specs=anywhere,
        scratch_shapes=[
            vmem((n_elem, width, bands), bf16), vmem((n_hop, n_grp, n_rows, width), bf16),
            vmem((width, width), bf16), vmem((width, bands), f32),
            vmem((n_grp, n_rows, slab), bf16), vmem((n_grp, n_rows, slab), bf16),
            vmem((2, n_rows, slab), bf16), vmem((2, n_rows, slab), bf16),
            vmem((2, 1, slab), f32),
            vmem((2, n_rows, half), f32), vmem((2, n_rows, half), f32),
            vmem((n_rows, half), f32), vmem((n_rows, half), f32), vmem((n_rows, half), f32),
            vmem((n_rows, half), bf16), vmem((n_rows, half), bf16),
            dma((7,)), dma((2, 2)), dma((2, 2)), dma((2, 2, PIECES)), dma((2, 2, PIECES)), dma((2,)),
            dma((3,)), dma((3,)), dma((3,)), dma((3,)), dma, dma,
            dma((1 + 2 * n_hop,)), dma((1 + 2 * n_hop,)),
            dma((n_elem, CHUNKS + 1)), dma((n_elem, CHUNKS + 1)),
            dma((n_elem, CHUNKS + 1)), dma((n_elem, CHUNKS + 1)), dma((bands // 256,)),
        ],
        compiler_params=pltpu.CompilerParams(
            collective_id=0, has_side_effects=True, vmem_limit_bytes=60 * 2 ** 20
        ),
        cost_estimate=pl.CostEstimate(
            flops=flops + 2 * n_elem * width * width * bands, bytes_accessed=2 ** 25, transcendentals=0
        ),
        name="hamiltonian",
    )(
        basis_values[0], basis_derivs[0], potential, hop_blocks[0], coeffs[0], counts, neighbours.T
    )
    return out[None]


def solution(mesh):
    placed = (
        P("elem", "grp", None),
        P("elem", "grp", None),
        P("elem", "grp"),
        P("elem", None, "grp", None),
        P("elem", None, "grp"),
        P(),
        P(),
    )
    fits = mesh.shape["elem"] == 8 and mesh.shape["grp"] == 4
    return jax.shard_map(
        local_kernels if fits else local,
        mesh=mesh, in_specs=placed, out_specs=P("elem", None, "grp"), check_vma=False,
    )
```
